256 devices in a mesh: head: 4 (over x), vocab: 32 (over y_lo, z, core), width: 2 (over y_hi).
Axes of the slice: x: 4, y: 4 (y_hi: 2, y_lo: 2; y = y_hi * 2 + y_lo), z: 8, core: 2. Of those that a mesh axis runs over, the one named last changes fastest.
Arguments:
- trunk_rows: bfloat16 [256, 6656], P(('vocab', 'width')), may hold values from -12 to 12
- res_weight: bfloat16 [4, 6656, 6656], P('head', None, ('width', 'vocab')), may hold values from -0.078125 to 0.078125
- res_bias: bfloat16 [4, 6656], P('head', ('width', 'vocab')), may hold values from -4 to 4
- lm_weight: bfloat16 [4, 6656, 20480], P('head', 'width', 'vocab'), may hold values from -0.08849741 to 0.08849741
- next_ids: int32 [260], replicated, may hold values from 0 to 20479
- valid_mask: int32 [260], replicated, may hold values 0 or 1
Outputs:
- trunk_grad: float32 [256, 6656], P(('vocab', 'width'))
- res_weight_grad: bfloat16 [4, 6656, 6656], P('head', None, ('width', 'vocab'))
- res_bias_grad: float32 [4, 6656], P('head', ('width', 'vocab'))
- lm_weight_grad: bfloat16 [4, 6656, 20480], P('head', 'width', 'vocab')
The draws below stay inside these ranges and needn't reach their ends.
All inputs are finite; a program needn't handle non-finite values.
Results may differ from the reference program's by a relative error of at most 0.01125.
Values may be sent and summed in bfloat16 or wider, within the bound.
No kernel may reach another device: no remote copies, remote signals or barrier semaphores. Data moves between devices by JAX's collectives and lax.ppermute only.
A program may use at most 128 MiB of HBM per device.

```python
import jax
import jax.numpy as jnp
from jax import lax

D = 6656
VOCAB = 20480
HEADS = 4
TOK = 256


def draw_trunk_rows(key, part):
    key = jax.random.fold_in(key, 3)
    values = jnp.clip(jax.random.normal(key, (TOK, D), jnp.float32), -6.0, 6.0)
    return values.astype(jnp.bfloat16)


def column_ramp(low_end, ratio):
    place = jnp.arange(VOCAB).astype(jnp.float32) / VOCAB
    return low_end * jnp.exp(jnp.log(ratio) * place)


def draw_lm_weight(key, part):
    key = jax.random.fold_in(key, 4)
    limit = 7.2 * D ** (-0.5)
    ramp = column_ramp(0.6, 1.6 / 0.6)
    values = jnp.clip(jax.random.normal(key, (HEADS, D, VOCAB), jnp.float32), -4.0, 4.0) * ramp[None, None, :] * D ** (-0.5)
    values = jnp.clip(values, -limit, limit)
    return values.astype(jnp.bfloat16)


def touch_ends(drawn, rng, low, largest):
    extent = drawn.shape
    spot = [jax.random.randint(jax.random.fold_in(rng, axis), (), 0, extent[axis]) for axis in range(len(extent))]
    drawn = drawn.at[tuple(spot)].set(low)
    longest = extent.index(max(extent))
    spot[longest] = (spot[longest] + 1) % extent[longest]
    return drawn.at[tuple(spot)].set(largest)


def block_levels(stream_key, extent, cuts, least, high):
    def one(position, shards_of):
        draws = jax.random.uniform(jax.random.fold_in(jax.random.fold_in(stream_key, 6), position), (shards_of,), jnp.float32, least / len(cuts), high / len(cuts))
        return jnp.repeat(jnp.exp(draws), extent[position] // shards_of).reshape((-1,) + (1,) * (len(extent) - position - 1))

    factor_of = one(*cuts[0])
    for cut in cuts[1:]:
        factor_of = factor_of * one(*cut)
    return factor_of


def noise(key, dims, width, bound, shards=(), kind=jnp.bfloat16):
    factor_of = block_levels(key, dims, shards, -0.22, 0.18) if shards else 1.0
    values = jax.random.normal(key, dims, jnp.float32) * width * factor_of
    return jnp.minimum(jnp.maximum(values, -bound), bound).astype(kind)


def setup_inputs(seed: int = 0) -> dict:
    splits = jax.random.split(jax.random.key(seed), 7)
    trunk_rows = draw_trunk_rows(jax.random.fold_in(splits[6], 71), 0)
    res_weight = noise(splits[1], (HEADS, D, D), D ** -0.5, 0.078125, ((0, 4), (2, 64)))
    res_bias = noise(splits[2], (HEADS, D), 1.0, 4.0, ((0, 4), (1, 64)))
    lm_weight = draw_lm_weight(jax.random.fold_in(splits[6], 71), 0)
    next_ids = touch_ends(jax.random.randint(splits[4], (TOK + HEADS,), 0, VOCAB), jax.random.fold_in(splits[4], 1), 0, VOCAB - 1).astype(jnp.int32)
    valid_mask = touch_ends((jax.random.randint(splits[5], (TOK + HEADS,), 0, 4) < 3).astype(jnp.int32), jax.random.fold_in(splits[5], 1), 0, 1)
    return dict(trunk_rows=trunk_rows, res_weight=res_weight, res_bias=res_bias, lm_weight=lm_weight, next_ids=next_ids, valid_mask=valid_mask)


loss_scale = 16.0

def silu_grad(value):
    sigma = jax.nn.sigmoid(value)
    return sigma * (1.0 + value * (1.0 - sigma))

def reference(trunk_rows, res_weight, res_bias, lm_weight, next_ids, valid_mask):
    trunk_sum = jnp.zeros((TOK, D), jnp.float32)
    columns = jnp.arange(VOCAB, dtype=jnp.int32)
    res_grads = []
    bias_grads = []
    lm_grads = []
    for head_idx in range(HEADS):
        pre_act = jnp.dot(trunk_rows, res_weight[head_idx], preferred_element_type=jnp.float32)
        pre_act = pre_act + res_bias[head_idx].astype(jnp.float32)[None, :]
        hidden = (trunk_rows.astype(jnp.float32) + jax.nn.silu(pre_act)).astype(jnp.bfloat16)
        logits = jnp.dot(hidden, lm_weight[head_idx], preferred_element_type=jnp.float32)
        top_val = lax.optimization_barrier(jnp.max(logits, axis=1, keepdims=True))
        row_exp = jnp.exp(logits - top_val)
        row_probs = row_exp / lax.optimization_barrier(jnp.sum(row_exp, axis=1, keepdims=True))
        tok_ids = next_ids[head_idx + 1:head_idx + 1 + TOK]
        live_rows = valid_mask[head_idx + 1:head_idx + 1 + TOK].astype(jnp.float32)
        onehot = (tok_ids[:, None] == columns[None, :]).astype(jnp.float32)
        head_scale = loss_scale * 0.8 ** head_idx
        grad_logits = (head_scale * live_rows[:, None] * (row_probs - onehot)).astype(jnp.bfloat16)
        lm_grads.append(lax.dot_general(hidden, grad_logits, (((0,), (0,)), ((), ())), preferred_element_type=jnp.float32).astype(jnp.bfloat16))
        hidden_grad = lax.dot_general(grad_logits, lm_weight[head_idx], (((1,), (1,)), ((), ())), preferred_element_type=jnp.float32)
        pre_grad = hidden_grad * silu_grad(pre_act)
        pre_round = pre_grad.astype(jnp.bfloat16)
        res_grads.append(lax.dot_general(trunk_rows, pre_round, (((0,), (0,)), ((), ())), preferred_element_type=jnp.float32).astype(jnp.bfloat16))
        bias_grads.append(lax.optimization_barrier(jnp.sum(pre_grad, axis=0)))
        trunk_sum = trunk_sum + hidden_grad + lax.dot_general(pre_round, res_weight[head_idx], (((1,), (1,)), ((), ())), preferred_element_type=jnp.float32)
    return (trunk_sum, jnp.stack(res_grads), jnp.stack(bias_grads), jnp.stack(lm_grads))
```

```python
import jax
import jax.numpy as jnp
from jax import lax
from jax.sharding import Mesh
from jax.sharding import PartitionSpec as P

loss_scale = 16.0
f32 = jnp.float32
bf16 = jnp.bfloat16
plane = ("ylo", "z")
plane_all = ("ylo", "z", "yhi")


def silu_grad(value):
    sigma = jax.nn.sigmoid(value)
    return sigma * (1.0 + value * (1.0 - sigma))


def swap(value, axis):
    return lax.ppermute(value, axis, [(0, 1), (1, 0)])


def exchange(value, axes):
    return lax.all_to_all(value, axes, 0, 0, tiled=True)


def dot(a, b, contract):
    return lax.dot_general(a, b, ((contract[0], contract[1]), ((), ())), preferred_element_type=f32)


def on_device(trunk_rows, res_weight, res_bias, lm_weight, next_ids, valid_mask):
    head = lax.axis_index("x")
    ylo, z, core, yhi = (lax.axis_index(a) for a in ("ylo", "z", "core", "yhi"))
    n_x = lax.axis_size("x")
    n_plane = lax.axis_size("ylo") * lax.axis_size("z")
    n_all = n_plane * lax.axis_size("yhi")
    rows, width = trunk_rows.shape
    quarter = width // n_x
    toks = n_all * rows

    res_own = res_weight[0].T
    cols = res_own.shape[0]
    pair = 2 * cols
    lm_own = lm_weight[0]
    half, vocab_width = lm_own.shape
    res_other = swap(res_own, "core")
    lm_other = swap(lm_own, "core")
    first = core == 0
    res_pair = jnp.concatenate(
        [jnp.where(first, res_own, res_other), jnp.where(first, res_other, res_own)], 0
    )
    bias_own = res_bias[0].astype(f32)
    bias_other = swap(bias_own, "core")
    bias_pair = jnp.concatenate(
        [jnp.where(first, bias_own, bias_other), jnp.where(first, bias_other, bias_own)]
    )

    mine = lax.dynamic_slice_in_dim(trunk_rows, head * quarter, quarter, 1)
    part = exchange(jnp.broadcast_to(mine[None], (n_all, rows, quarter)), plane_all)
    part = part.reshape(toks, quarter)
    trunk = exchange(jnp.broadcast_to(part[None], (n_x, toks, quarter)), "x")

    chip = ylo * lax.axis_size("z") + z
    per_quarter = quarter // pair
    block = yhi * n_plane + chip
    pre = bias_pair[:, None]
    for q in range(n_x):
        pre = pre + dot(res_pair[:, q * quarter : (q + 1) * quarter], trunk[q], ((1,), (1,)))
    own_cols = lax.dynamic_slice(
        trunk, (block // per_quarter, 0, (block % per_quarter) * pair), (1, toks, pair)
    )[0].T
    hidden = (own_cols.astype(f32) + jax.nn.silu(pre)).astype(bf16)
    hidden_half = exchange(
        jnp.broadcast_to(hidden[None], (n_plane, pair, toks)), plane
    ).reshape(half, toks)

    logits_own = dot(hidden_half, lm_own, ((0,), (0,)))
    logits_other = dot(hidden_half, lm_other, ((0,), (0,)))
    logits_own = logits_own + swap(logits_own, "yhi")
    logits_other = logits_other + swap(logits_other, "yhi")
    top = jnp.maximum(jnp.max(logits_own, axis=1), jnp.max(logits_other, axis=1))
    exp_own = jnp.exp(logits_own - top[:, None])
    exp_other = jnp.exp(logits_other - top[:, None])
    total = jnp.sum(exp_own, axis=1) + jnp.sum(exp_other, axis=1)
    stats = jnp.stack([top, total])
    stats = exchange(jnp.broadcast_to(stats[None], (n_plane, 2, toks)), plane)
    all_top = jnp.max(stats[:, 0], axis=0)
    all_total = jnp.sum(stats[:, 1] * jnp.exp(stats[:, 0] - all_top[None]), axis=0)

    def own_tokens(values):
        values = lax.dynamic_slice_in_dim(values, head + 1, 2 * toks)
        values = values.reshape(n_plane, 2, toks // n_plane)
        return lax.dynamic_index_in_dim(values, core, 1, keepdims=False).reshape(toks)

    tok_ids = own_tokens(next_ids)
    live = own_tokens(valid_mask).astype(f32)
    scale = loss_scale * jnp.power(jnp.float32(0.8), head.astype(f32)) * live
    ratio = scale * jnp.exp(top - all_top) / all_total
    lanes = lax.broadcasted_iota(jnp.int32, (1, vocab_width), 1)

    def grad_of(exps, owner):
        local = tok_ids - (chip * 2 + owner) * vocab_width
        onehot = (local[:, None] == lanes).astype(f32)
        return (ratio[:, None] * exps - scale[:, None] * onehot).astype(bf16)

    grad_own = grad_of(exp_own, core)
    grad_other = grad_of(exp_other, 1 - core)

    part_grad = dot(lm_own, grad_own, ((1,), (1,))) + dot(lm_other, grad_other, ((1,), (1,)))
    parts = exchange(part_grad.astype(bf16).reshape(n_plane, pair, toks), plane)
    hidden_grad = jnp.sum(parts.astype(f32), axis=0)
    pre_grad = hidden_grad * silu_grad(pre)
    pre_round = pre_grad.astype(bf16)

    outs = [
        dot(pre_round, res_pair[:, q * quarter : (q + 1) * quarter], ((0,), (0,)))
        for q in range(n_x)
    ]
    partial = jnp.stack(outs)
    spot = (block // per_quarter, 0, (block % per_quarter) * pair)
    direct = lax.dynamic_slice(partial, spot, (1, toks, pair)) + hidden_grad.T[None]
    partial = lax.dynamic_update_slice(partial, direct, spot).astype(bf16)
    by_x = jnp.sum(exchange(partial, "x").astype(f32), axis=0).astype(bf16)
    by_plane = exchange(by_x.reshape(n_all, rows, quarter), plane_all)
    summed = jnp.sum(by_plane.astype(f32), axis=0)
    quarters = exchange(jnp.broadcast_to(summed[None], (n_x, rows, quarter)), "x")
    trunk_grad = quarters.transpose(1, 0, 2).reshape(rows, width)

    hidden_both = jnp.concatenate([hidden_half, swap(hidden_half, "core")], 1)
    grad_both = jnp.concatenate([grad_own, swap(grad_other, "core")], 0)
    lm_grad = dot(hidden_both, grad_both, ((1,), (0,))).astype(bf16)
    pre_own = lax.dynamic_slice_in_dim(pre_grad, core * cols, cols, 0)
    pre_sibling = swap(lax.dynamic_slice_in_dim(pre_grad, (1 - core) * cols, cols, 0), "core")
    bias_grad = jnp.sum(pre_own, axis=1) + jnp.sum(pre_sibling, axis=1)
    pre_both = jnp.concatenate([pre_own, pre_sibling], 1).astype(bf16)
    trunk_both = jnp.concatenate([trunk, swap(trunk, "core")], 1)
    res_grad = jnp.concatenate(
        [dot(pre_both, trunk_both[q], ((1,), (0,))) for q in range(n_x)], 1
    ).astype(bf16)
    return (trunk_grad, res_grad.T[None], bias_grad[None], lm_grad[None])


def solution(mesh):
    fine = Mesh(mesh.devices.reshape(4, 2, 8, 2, 2), ("x", "ylo", "z", "core", "yhi"))
    vocab = ("ylo", "z", "core")
    in_specs = (
        P((*vocab, "yhi"), None),
        P("x", None, ("yhi", *vocab)),
        P("x", ("yhi", *vocab)),
        P("x", "yhi", vocab),
        P(),
        P(),
    )
    out_specs = (
        P((*vocab, "yhi"), None),
        P("x", None, ("yhi", *vocab)),
        P("x", ("yhi", *vocab)),
        P("x", "yhi", vocab),
    )
    return jax.shard_map(
        on_device, mesh=fine, in_specs=in_specs, out_specs=out_specs, check_vma=False
    )
```

```python
import jax
import jax.numpy as jnp
from jax import lax
from jax.experimental import pallas as pl
from jax.experimental.pallas import tpu as pltpu
from jax.sharding import Mesh
from jax.sharding import PartitionSpec as P

loss_scale = 16.0
f32 = jnp.float32
bf16 = jnp.bfloat16
plane = ("ylo", "z")
plane_all = ("ylo", "z", "yhi")


def silu_grad(value):
    sigma = jax.nn.sigmoid(value)
    return sigma * (1.0 + value * (1.0 - sigma))


def swap(value, axis):
    return lax.ppermute(value, axis, [(0, 1), (1, 0)])


def exchange(value, axes):
    return lax.all_to_all(value, axes, 0, 0, tiled=True)


def dot(a, b, contract):
    return lax.dot_general(a, b, ((contract[0], contract[1]), ((), ())), preferred_element_type=f32)


def vocab_product(lm_a, lm_b, rows_a, rows_b, dtype):
    half, columns = lm_a.shape
    toks = rows_a.shape[0]
    step = half // 2

    def kernel(a_ref, b_ref, ra_ref, rb_ref, out_ref):
        total = dot(a_ref[...], ra_ref[...], ((1,), (1,)))
        total = total + dot(b_ref[...], rb_ref[...], ((1,), (1,)))
        out_ref[...] = total.astype(out_ref.dtype)

    weights = pl.BlockSpec((step, columns), lambda i: (i, 0))
    whole = pl.BlockSpec((toks, columns), lambda i: (0, 0))
    return pl.pallas_call(
        kernel,
        grid=(half // step,),
        in_specs=[weights, weights, whole, whole],
        out_specs=pl.BlockSpec((step, toks), lambda i: (i, 0)),
        out_shape=jax.ShapeDtypeStruct((half, toks), dtype),
        cost_estimate=pl.CostEstimate(
            flops=4 * half * columns * toks,
            bytes_accessed=4 * half * columns + 4 * half * toks,
            transcendentals=0,
        ),
        compiler_params=pltpu.CompilerParams(vmem_limit_bytes=24 * 2**20),
    )(lm_a, lm_b, rows_a, rows_b)


def combine(stats, own, product, target_cols):
    half, toks = product.shape
    step = half // 2

    def kernel(stats_ref, own_ref, product_ref, target_ref, out_ref, ratio_ref):
        tops, rests, targets = stats_ref[:, 0, :], stats_ref[:, 1, :], stats_ref[:, 2, :]
        top, scale = own_ref[0:1, :], own_ref[1:2, :]
        all_top = jnp.max(tops, axis=0, keepdims=True)
        weight = jnp.exp(tops - all_top)
        rest = jnp.sum(rests * weight, axis=0, keepdims=True)
        total = rest + jnp.sum(targets * weight, axis=0, keepdims=True)
        ratio = scale * jnp.exp(top - all_top) / total
        ratio_ref[...] = ratio
        value = product_ref[...] * ratio - target_ref[...].astype(f32) * (scale * rest / total)
        out_ref[...] = value.astype(out_ref.dtype)

    rows = pl.BlockSpec((step, toks), lambda i: (i, 0))
    return pl.pallas_call(
        kernel,
        grid=(half // step,),
        in_specs=[
            pl.BlockSpec(stats.shape, lambda i: (0, 0, 0)),
            pl.BlockSpec(own.shape, lambda i: (0, 0)),
            rows,
            rows,
        ],
        out_specs=[rows, pl.BlockSpec((1, toks), lambda i: (0, 0))],
        out_shape=[
            jax.ShapeDtypeStruct((half, toks), bf16),
            jax.ShapeDtypeStruct((1, toks), f32),
        ],
        cost_estimate=pl.CostEstimate(
            flops=4 * half * toks, bytes_accessed=8 * half * toks, transcendentals=0
        ),
    )(stats, own, product, target_cols)


def on_device(trunk_rows, res_weight, res_bias, lm_weight, next_ids, valid_mask):
    head = lax.axis_index("x")
    ylo, z, core, yhi = (lax.axis_index(a) for a in ("ylo", "z", "core", "yhi"))
    n_x = lax.axis_size("x")
    n_plane = lax.axis_size("ylo") * lax.axis_size("z")
    n_all = n_plane * lax.axis_size("yhi")
    rows, width = trunk_rows.shape
    toks = n_all * rows

    res_own = res_weight[0].T
    cols = res_own.shape[0]
    pair = 2 * cols
    lm_own = lm_weight[0]
    half, vocab_width = lm_own.shape
    res_other = swap(res_own, "core")
    lm_other = swap(lm_own, "core")
    first = core == 0
    res_pair = jnp.concatenate(
        [jnp.where(first, res_own, res_other), jnp.where(first, res_other, res_own)], 0
    )
    bias_own = res_bias[0].astype(f32)
    bias_other = swap(bias_own, "core")
    bias_pair = jnp.concatenate(
        [jnp.where(first, bias_own, bias_other), jnp.where(first, bias_other, bias_own)]
    )

    chip = ylo * lax.axis_size("z") + z
    block = yhi * n_plane + chip
    odd = head % 2
    half_cols = width // 2
    quarter = half_cols // 2
    iota_r = lax.broadcasted_iota(jnp.int32, (pair, half_cols), 0)
    iota_c = lax.broadcasted_iota(jnp.int32, (pair, half_cols), 1)

    def aug(side):
        weights = jnp.where(side == 0, res_pair[:, :half_cols], res_pair[:, half_cols:])
        select = (iota_r + block * pair == iota_c + side * half_cols).astype(bf16)
        return jnp.concatenate([weights, select], 0)

    near, far = aug(odd), aug(1 - odd)

    def shift(value, step):
        return lax.ppermute(value, "x", [(i, (i + step) % n_x) for i in range(n_x)])

    mine = lax.dynamic_slice_in_dim(trunk_rows, odd * half_cols, half_cols, 1)
    part = exchange(jnp.broadcast_to(mine[None], (n_all, rows, half_cols)), plane_all)
    part = part.reshape(toks, half_cols)

    def own_tokens(values):
        values = lax.dynamic_slice_in_dim(values, head + 1, 2 * toks)
        values = values.reshape(n_plane, 2, toks // n_plane)
        return lax.dynamic_index_in_dim(values, core, 1, keepdims=False).reshape(toks)

    tok_ids = own_tokens(next_ids)
    live = own_tokens(valid_mask).astype(f32)
    scale = loss_scale * jnp.power(jnp.float32(0.8), head.astype(f32)) * live
    lanes = lax.broadcasted_iota(jnp.int32, (1, vocab_width), 1)

    def onehot(owner):
        return (tok_ids - (chip * 2 + owner) * vocab_width)[:, None] == lanes

    hot_own, hot_other = onehot(core), onehot(1 - core)
    target_cols = vocab_product(
        lm_own, lm_other, hot_own.astype(bf16), hot_other.astype(bf16), bf16
    )
    from_right = shift(part[:, :quarter], -1)
    from_left = shift(part[:, quarter:], 1)

    both = dot(near, part, ((1,), (1,)))
    both = both + dot(far[:, :quarter], from_right, ((1,), (1,)))
    both = both + dot(far[:, quarter:], from_left, ((1,), (1,)))
    pre = both[:pair] + bias_pair[:, None]
    hidden = (both[pair:] + jax.nn.silu(pre)).astype(bf16)
    hidden_half = exchange(
        jnp.broadcast_to(hidden[None], (n_plane, pair, toks)), plane
    ).reshape(half, toks)
    target_cols, hidden_half = lax.optimization_barrier((target_cols, hidden_half))

    logits_own = dot(hidden_half, lm_own, ((0,), (0,)))
    logits_other = dot(hidden_half, lm_other, ((0,), (0,)))
    logits_own = logits_own + swap(logits_own, "yhi")
    logits_other = logits_other + swap(logits_other, "yhi")
    top = jnp.maximum(jnp.max(logits_own, axis=1), jnp.max(logits_other, axis=1))
    exp_own = jnp.exp(logits_own - top[:, None])
    exp_other = jnp.exp(logits_other - top[:, None])
    rest_own = jnp.where(hot_own, 0.0, exp_own)
    rest_other = jnp.where(hot_other, 0.0, exp_other)
    rest = jnp.sum(rest_own, axis=1) + jnp.sum(rest_other, axis=1)
    at_target = jnp.sum(jnp.where(hot_own, exp_own, 0.0), axis=1) + jnp.sum(
        jnp.where(hot_other, exp_other, 0.0), axis=1
    )
    stats = jnp.stack([top, rest, at_target])
    stats = exchange(jnp.broadcast_to(stats[None], (n_plane, 3, toks)), plane)
    part_grad = vocab_product(
        lm_own, lm_other, rest_own.astype(bf16), rest_other.astype(bf16), f32
    )
    part_grad, ratio = combine(stats, jnp.stack([top, scale]), part_grad, target_cols)
    ratio = ratio[0]
    parts = exchange(part_grad.reshape(n_plane, pair, toks), plane)
    hidden_grad = jnp.sum(parts.astype(f32), axis=0)
    pre_grad = hidden_grad * silu_grad(pre)
    pre_round = pre_grad.astype(bf16)

    both_grad = jnp.concatenate([pre_round, hidden_grad.astype(bf16)], 0)
    keep = dot(both_grad, near, ((0,), (0,)))
    give_left = dot(both_grad, far[:, :quarter], ((0,), (0,))).astype(bf16)
    give_right = dot(both_grad, far[:, quarter:], ((0,), (0,))).astype(bf16)
    got_left = shift(give_right, 1)
    got_right = shift(give_left, -1)
    by_x = jnp.concatenate(
        [keep[:, :quarter] + got_right.astype(f32), keep[:, quarter:] + got_left.astype(f32)], 1
    ).astype(bf16)
    by_plane = exchange(by_x.reshape(n_all, rows, half_cols), plane_all)
    summed = jnp.sum(by_plane.astype(f32), axis=0)
    here = summed + shift(summed, 2)
    there = shift(summed, 1) + shift(summed, -1)
    trunk_grad = jnp.concatenate(
        [jnp.where(odd == 0, here, there), jnp.where(odd == 0, there, here)], 1
    )

    def grad_of(exps, hot):
        return jnp.where(hot, ratio[:, None] * exps - scale[:, None], ratio[:, None] * exps).astype(
            bf16
        )

    grad_own = grad_of(exp_own, hot_own)
    grad_other = grad_of(exp_other, hot_other)
    hidden_both = jnp.concatenate([hidden_half, swap(hidden_half, "core")], 1)
    grad_both = jnp.concatenate([grad_own, swap(grad_other, "core")], 0)
    lm_grad = dot(hidden_both, grad_both, ((1,), (0,))).astype(bf16)
    pre_own = lax.dynamic_slice_in_dim(pre_grad, core * cols, cols, 0)
    pre_sibling = swap(lax.dynamic_slice_in_dim(pre_grad, (1 - core) * cols, cols, 0), "core")
    bias_grad = jnp.sum(pre_own, axis=1) + jnp.sum(pre_sibling, axis=1)
    pre_both = jnp.concatenate([pre_own, pre_sibling], 1).astype(bf16)

    def with_sibling(value):
        return jnp.concatenate([value, swap(value, "core")], 0)

    res_near = dot(pre_both, with_sibling(part), ((1,), (0,))).astype(bf16)
    res_far = jnp.concatenate(
        [dot(pre_both, with_sibling(v), ((1,), (0,))) for v in (from_right, from_left)], 1
    ).astype(bf16)
    res_grad = jnp.concatenate(
        [jnp.where(odd == 0, res_near, res_far), jnp.where(odd == 0, res_far, res_near)], 1
    )
    return (trunk_grad, res_grad.T[None], bias_grad[None], lm_grad[None])


def solution(mesh):
    fine = Mesh(mesh.devices.reshape(4, 2, 8, 2, 2), ("x", "ylo", "z", "core", "yhi"))
    vocab = ("ylo", "z", "core")
    in_specs = (
        P((*vocab, "yhi"), None),
        P("x", None, ("yhi", *vocab)),
        P("x", ("yhi", *vocab)),
        P("x", "yhi", vocab),
        P(),
        P(),
    )
    out_specs = (
        P((*vocab, "yhi"), None),
        P("x", None, ("yhi", *vocab)),
        P("x", ("yhi", *vocab)),
        P("x", "yhi", vocab),
    )
    return jax.shard_map(
        on_device, mesh=fine, in_specs=in_specs, out_specs=out_specs, check_vma=False
    )
```

```python
import jax
import jax.numpy as jnp
from jax import lax
from jax.experimental import pallas as pl
from jax.experimental.pallas import tpu as pltpu
from jax.sharding import Mesh
from jax.sharding import PartitionSpec as P

loss_scale = 16.0
int16_top = 32767.0
ln2 = 0.6931471805599453
vmem_bytes = 60 * 2**20
f32 = jnp.float32
bf16 = jnp.bfloat16
plane = ("ylo", "z")
plane_all = ("ylo", "z", "yhi")


def silu_grad(value):
    sigma = jax.nn.sigmoid(value)
    return sigma * (1.0 + value * (1.0 - sigma))


def swap(value, axis):
    return lax.ppermute(value, axis, [(0, 1), (1, 0)])


def exchange(value, axes):
    return lax.all_to_all(value, axes, 0, 0, tiled=True)


def dot(a, b, contract):
    return lax.dot_general(a, b, ((contract[0], contract[1]), ((), ())), preferred_element_type=f32)


def vocab_product(lm_a, lm_b, rows_a, rows_b, dtype):
    half, columns = lm_a.shape
    toks = rows_a.shape[0]
    step = half // 2

    def kernel(a_ref, b_ref, ra_ref, rb_ref, out_ref):
        total = dot(a_ref[...], ra_ref[...], ((1,), (1,)))
        total = total + dot(b_ref[...], rb_ref[...], ((1,), (1,)))
        out_ref[...] = total.astype(out_ref.dtype)

    weights = pl.BlockSpec((step, columns), lambda i: (i, 0))
    whole = pl.BlockSpec((toks, columns), lambda i: (0, 0))
    return pl.pallas_call(
        kernel,
        grid=(half // step,),
        in_specs=[weights, weights, whole, whole],
        out_specs=pl.BlockSpec((step, toks), lambda i: (i, 0)),
        out_shape=jax.ShapeDtypeStruct((half, toks), dtype),
        cost_estimate=pl.CostEstimate(
            flops=4 * half * columns * toks,
            bytes_accessed=4 * half * columns + 4 * half * toks,
            transcendentals=0,
        ),
        compiler_params=pltpu.CompilerParams(vmem_limit_bytes=vmem_bytes),
    )(lm_a, lm_b, rows_a, rows_b)


def vocab_logits(hidden, lm_a, lm_b):
    half, columns = lm_a.shape
    toks = hidden.shape[1]
    step = half // 2
    lanes = 128

    def kernel(h_ref, a_ref, b_ref, out_ref, coded_ref):
        part_a = dot(h_ref[...], a_ref[...], ((0,), (0,)))
        part_b = dot(h_ref[...], b_ref[...], ((0,), (0,)))

        @pl.when(pl.program_id(0) == 0)
        def _():
            out_ref[:, :columns] = part_a
            out_ref[:, columns:] = part_b

        @pl.when(pl.program_id(0) > 0)
        def _():
            value = out_ref[...] + jnp.concatenate([part_a, part_b], 1)
            out_ref[...] = value
            size = jnp.max(jnp.abs(value), axis=1, keepdims=True)
            power = jnp.ceil(jnp.log(jnp.maximum(size, 1e-30)) * (1.0 / ln2))
            code = jnp.floor(value * (int16_top * jnp.exp(power * -ln2)) + 0.5)
            code = jnp.clip(code, -int16_top, int16_top)
            coded_ref[:, : 2 * columns] = code.astype(jnp.int32).astype(jnp.int16)
            power = jnp.broadcast_to(power, (toks, lanes))
            coded_ref[:, 2 * columns :] = power.astype(jnp.int32).astype(jnp.int16)

    weights = pl.BlockSpec((step, columns), lambda i: (i, 0))
    return pl.pallas_call(
        kernel,
        grid=(half // step,),
        in_specs=[pl.BlockSpec((step, toks), lambda i: (i, 0)), weights, weights],
        out_specs=[
            pl.BlockSpec((toks, 2 * columns), lambda i: (0, 0)),
            pl.BlockSpec((toks, 2 * columns + lanes), lambda i: (0, 0)),
        ],
        out_shape=[
            jax.ShapeDtypeStruct((toks, 2 * columns), f32),
            jax.ShapeDtypeStruct((toks, 2 * columns + lanes), jnp.int16),
        ],
        cost_estimate=pl.CostEstimate(
            flops=4 * half * columns * toks,
            bytes_accessed=4 * half * columns + 2 * half * toks,
            transcendentals=0,
        ),
        compiler_params=pltpu.CompilerParams(vmem_limit_bytes=vmem_bytes),
    )(hidden, lm_a, lm_b)


def combine(stats, own, product, target_cols):
    half, toks = product.shape
    step = half // 2

    def kernel(stats_ref, own_ref, product_ref, target_ref, out_ref, ratio_ref):
        tops, rests, targets = stats_ref[:, 0, :], stats_ref[:, 1, :], stats_ref[:, 2, :]
        top, scale = own_ref[0:1, :], own_ref[1:2, :]
        all_top = jnp.max(tops, axis=0, keepdims=True)
        weight = jnp.exp(tops - all_top)
        rest = jnp.sum(rests * weight, axis=0, keepdims=True)
        total = rest + jnp.sum(targets * weight, axis=0, keepdims=True)
        ratio = scale * jnp.exp(top - all_top) / total
        ratio_ref[...] = ratio
        value = product_ref[...] * ratio - target_ref[...].astype(f32) * (scale * rest / total)
        out_ref[...] = value.astype(out_ref.dtype)

    rows = pl.BlockSpec((step, toks), lambda i: (i, 0))
    return pl.pallas_call(
        kernel,
        grid=(half // step,),
        in_specs=[
            pl.BlockSpec(stats.shape, lambda i: (0, 0, 0)),
            pl.BlockSpec(own.shape, lambda i: (0, 0)),
            rows,
            rows,
        ],
        out_specs=[rows, pl.BlockSpec((1, toks), lambda i: (0, 0))],
        out_shape=[
            jax.ShapeDtypeStruct((half, toks), bf16),
            jax.ShapeDtypeStruct((1, toks), f32),
        ],
        cost_estimate=pl.CostEstimate(
            flops=4 * half * toks, bytes_accessed=8 * half * toks, transcendentals=0
        ),
        compiler_params=pltpu.CompilerParams(vmem_limit_bytes=vmem_bytes),
    )(stats, own, product, target_cols)


def on_device(trunk_rows, res_weight, res_bias, lm_weight, next_ids, valid_mask):
    head = lax.axis_index("x")
    ylo, z, core, yhi = (lax.axis_index(a) for a in ("ylo", "z", "core", "yhi"))
    n_x = lax.axis_size("x")
    n_plane = lax.axis_size("ylo") * lax.axis_size("z")
    n_all = n_plane * lax.axis_size("yhi")
    rows, width = trunk_rows.shape
    toks = n_all * rows

    res_own = res_weight[0].T
    cols = res_own.shape[0]
    pair = 2 * cols
    lm_own = lm_weight[0]
    half, vocab_width = lm_own.shape
    res_other = swap(res_own, "core")
    lm_other = swap(lm_own, "core")
    first = core == 0
    res_pair = jnp.concatenate(
        [jnp.where(first, res_own, res_other), jnp.where(first, res_other, res_own)], 0
    )
    bias_own = res_bias[0].astype(f32)
    bias_other = swap(bias_own, "core")
    bias_pair = jnp.concatenate(
        [jnp.where(first, bias_own, bias_other), jnp.where(first, bias_other, bias_own)]
    )

    chip = ylo * lax.axis_size("z") + z
    block = yhi * n_plane + chip
    odd = head % 2
    half_cols = width // 2
    quarter = half_cols // 2
    iota_r = lax.broadcasted_iota(jnp.int32, (pair, half_cols), 0)
    iota_c = lax.broadcasted_iota(jnp.int32, (pair, half_cols), 1)

    select = jnp.concatenate(
        [(iota_r + block * pair == iota_c + side * half_cols).astype(bf16) for side in (0, 1)], 1
    )
    res_aug = jnp.concatenate([res_pair, select], 0)
    near = lax.dynamic_slice_in_dim(res_aug, odd * half_cols, half_cols, 1)
    far = lax.dynamic_slice_in_dim(res_aug, (1 - odd) * half_cols, half_cols, 1)

    def shift(value, step):
        return lax.ppermute(value, "x", [(i, (i + step) % n_x) for i in range(n_x)])

    line = ("ylo", "yhi")
    n_z = lax.axis_size("z")
    n_y = lax.axis_size("ylo") * lax.axis_size("yhi")
    y = yhi * lax.axis_size("ylo") + ylo

    def z_shift(value, step):
        return lax.ppermute(value, "z", [(i, (i + step) % n_z) for i in range(n_z)])

    def line_index(at):
        return at % 2 * 2 + at // 2

    def y_shift(value, step):
        pairs = [(line_index(i), line_index((i + step) % n_y)) for i in range(n_y)]
        return lax.ppermute(value, line, pairs)

    def place(buffer, block, at, row=0, col=0):
        return lax.dynamic_update_slice(buffer, block[None], (at, row, col))

    up = down = trunk_rows
    seen = place(jnp.zeros((n_z, rows, width), bf16), trunk_rows, z)
    for step in range(1, n_z // 2):
        up, down = z_shift(up, 1), z_shift(down, -1)
        seen = place(seen, up, (z - step) % n_z)
        seen = place(seen, down, (z + step) % n_z)
    up, down = z_shift(up[:, :half_cols], 1), z_shift(down[:, half_cols:], -1)
    seen = place(seen, up, (z + n_z // 2) % n_z)
    seen = place(seen, down, (z + n_z // 2) % n_z, 0, half_cols)

    seen = seen.reshape(n_z * rows, width)
    cut = n_z * rows // 2
    trunk = place(jnp.zeros((n_y, n_z * rows, width), bf16), seen, y)
    up, down = y_shift(seen, 1), y_shift(seen, -1)
    trunk = place(trunk, up, (y - 1) % n_y)
    trunk = place(trunk, down, (y + 1) % n_y)
    trunk = place(trunk, y_shift(up[:cut], 1), (y + 2) % n_y)
    trunk = place(trunk, y_shift(down[cut:], -1), (y + 2) % n_y, cut)
    trunk = trunk.reshape(toks, width)

    def own_tokens(values):
        values = lax.dynamic_slice_in_dim(values, head + 1, 2 * toks)
        values = values.reshape(lax.axis_size("ylo"), n_z, 2, lax.axis_size("yhi"), rows)
        values = lax.dynamic_index_in_dim(values, core, 2, keepdims=False)
        return values.transpose(2, 0, 1, 3).reshape(toks)

    tok_ids = own_tokens(next_ids)
    live = own_tokens(valid_mask).astype(f32)
    scale = loss_scale * jnp.power(jnp.float32(0.8), head.astype(f32)) * live
    lanes = lax.broadcasted_iota(jnp.int32, (1, vocab_width), 1)

    def onehot(owner):
        return (tok_ids - (chip * 2 + owner) * vocab_width)[:, None] == lanes

    hot_own, hot_other = onehot(core), onehot(1 - core)
    target_cols = vocab_product(
        lm_own, lm_other, hot_own.astype(bf16), hot_other.astype(bf16), bf16
    )
    both = dot(res_aug, trunk, ((1,), (1,)))
    pre = both[:pair] + bias_pair[:, None]
    hidden = (both[pair:] + jax.nn.silu(pre)).astype(bf16)
    hidden_half = exchange(
        jnp.broadcast_to(hidden[None], (n_plane, pair, toks)), plane
    ).reshape(half, toks)
    target_cols, hidden_half = lax.optimization_barrier((target_cols, hidden_half))

    logits, coded = vocab_logits(hidden_half, lm_own, lm_other)
    coded = swap(coded, "yhi").astype(f32)
    logits = logits + coded[:, : 2 * vocab_width] * (
        jnp.exp(coded[:, 2 * vocab_width : 2 * vocab_width + 1] * ln2) * (1.0 / int16_top)
    )
    logits_own, logits_other = logits[:, :vocab_width], logits[:, vocab_width:]
    top = jnp.maximum(jnp.max(logits_own, axis=1), jnp.max(logits_other, axis=1))
    exp_own = jnp.exp(logits_own - top[:, None])
    exp_other = jnp.exp(logits_other - top[:, None])
    rest_own = jnp.where(hot_own, 0.0, exp_own)
    rest_other = jnp.where(hot_other, 0.0, exp_other)
    rest = jnp.sum(rest_own, axis=1) + jnp.sum(rest_other, axis=1)
    at_target = jnp.sum(jnp.where(hot_own, exp_own, 0.0), axis=1) + jnp.sum(
        jnp.where(hot_other, exp_other, 0.0), axis=1
    )
    stats = jnp.stack([top, rest, at_target])
    stats = exchange(jnp.broadcast_to(stats[None], (n_plane, 3, toks)), plane)
    part_grad = vocab_product(
        lm_own, lm_other, rest_own.astype(bf16), rest_other.astype(bf16), f32
    )
    part_grad, ratio = combine(stats, jnp.stack([top, scale]), part_grad, target_cols)
    ratio = ratio[0]
    parts = exchange(part_grad.reshape(n_plane, pair, toks), plane)
    hidden_grad = jnp.sum(parts.astype(f32), axis=0)
    pre_grad = hidden_grad * silu_grad(pre)
    pre_round = pre_grad.astype(bf16)

    both_grad = jnp.concatenate([pre_round, hidden_grad.astype(bf16)], 0)
    given = dot(both_grad, far, ((0,), (0,))).astype(bf16)
    got_left = shift(given[:, quarter:], 1)
    got_right = shift(given[:, :quarter], -1)
    keep = dot(both_grad, near, ((0,), (0,)))
    by_x = jnp.concatenate(
        [keep[:, :quarter] + got_right.astype(f32), keep[:, quarter:] + got_left.astype(f32)], 1
    ).astype(bf16)
    by_x = by_x.reshape(n_y, n_z * rows, half_cols)
    by_y = lax.dynamic_index_in_dim(by_x, y, 0, keepdims=False).astype(f32)
    for flip in (1, 3, 2):
        sent = lax.dynamic_index_in_dim(by_x, y ^ flip, 0, keepdims=False)
        pairs = [(line_index(i), line_index(i ^ flip)) for i in range(n_y)]
        got = lax.ppermute(sent, line, pairs)
        by_y = by_y + got.astype(f32)
    by_z = exchange(by_y.astype(bf16).reshape(n_z, rows, half_cols), "z")
    summed = jnp.sum(by_z.astype(f32), axis=0)
    here = summed + shift(summed, 2)
    there = shift(summed, 1) + shift(summed, -1)
    trunk_grad = jnp.concatenate(
        [jnp.where(odd == 0, here, there), jnp.where(odd == 0, there, here)], 1
    )

    def grad_of(exps, hot):
        return jnp.where(hot, ratio[:, None] * exps - scale[:, None], ratio[:, None] * exps).astype(
            bf16
        )

    grad_own = grad_of(exp_own, hot_own)
    grad_other = grad_of(exp_other, hot_other)
    hidden_both = jnp.concatenate([hidden_half, swap(hidden_half, "core")], 1)
    grad_both = jnp.concatenate([grad_own, swap(grad_other, "core")], 0)
    lm_grad = dot(hidden_both, grad_both, ((1,), (0,))).astype(bf16)
    pre_own = lax.dynamic_slice_in_dim(pre_grad, core * cols, cols, 0)
    pre_sibling = swap(lax.dynamic_slice_in_dim(pre_grad, (1 - core) * cols, cols, 0), "core")
    bias_grad = jnp.sum(pre_own, axis=1) + jnp.sum(pre_sibling, axis=1)
    pre_both = jnp.concatenate([pre_own, pre_sibling], 1).astype(bf16)

    trunk_both = jnp.concatenate([trunk, swap(trunk, "core")], 0)
    res_grad = dot(pre_both, trunk_both, ((1,), (0,))).astype(bf16)
    return (trunk_grad, res_grad.T[None], bias_grad[None], lm_grad[None])


def solution(mesh):
    fine = Mesh(mesh.devices.reshape(4, 2, 8, 2, 2), ("x", "ylo", "z", "core", "yhi"))
    vocab = ("ylo", "z", "core")
    in_specs = (
        P((*vocab, "yhi"), None),
        P("x", None, ("yhi", *vocab)),
        P("x", ("yhi", *vocab)),
        P("x", "yhi", vocab),
        P(),
        P(),
    )
    out_specs = (
        P((*vocab, "yhi"), None),
        P("x", None, ("yhi", *vocab)),
        P("x", ("yhi", *vocab)),
        P("x", "yhi", vocab),
    )
    return jax.shard_map(
        on_device, mesh=fine, in_specs=in_specs, out_specs=out_specs, check_vma=False
    )
```

```python
import jax
import jax.numpy as jnp
from jax import lax
from jax.experimental import pallas as pl
from jax.experimental.pallas import tpu as pltpu
from jax.sharding import Mesh
from jax.sharding import PartitionSpec as P

loss_scale = 16.0
int16_top = 32767.0
ln2 = 0.6931471805599453
vmem_bytes = 60 * 2**20
f32 = jnp.float32
bf16 = jnp.bfloat16
plane = ("ylo", "z")
plane_all = ("ylo", "z", "yhi")


def silu_grad(value):
    sigma = jax.nn.sigmoid(value)
    return sigma * (1.0 + value * (1.0 - sigma))


def swap(value, axis):
    return lax.ppermute(value, axis, [(0, 1), (1, 0)])


def exchange(value, axes):
    return lax.all_to_all(value, axes, 0, 0, tiled=True)


def dot(a, b, contract):
    return lax.dot_general(a, b, ((contract[0], contract[1]), ((), ())), preferred_element_type=f32)


def vocab_product(lm_a, lm_b, rows_a, rows_b, dtype):
    half, columns = lm_a.shape
    toks = rows_a.shape[0]
    step = half // 2

    def kernel(a_ref, b_ref, ra_ref, rb_ref, out_ref):
        total = dot(a_ref[...], ra_ref[...], ((1,), (1,)))
        total = total + dot(b_ref[...], rb_ref[...], ((1,), (1,)))
        out_ref[...] = total.astype(out_ref.dtype)

    weights = pl.BlockSpec((step, columns), lambda i: (i, 0))
    whole = pl.BlockSpec((toks, columns), lambda i: (0, 0))
    return pl.pallas_call(
        kernel,
        grid=(half // step,),
        in_specs=[weights, weights, whole, whole],
        out_specs=pl.BlockSpec((step, toks), lambda i: (i, 0)),
        out_shape=jax.ShapeDtypeStruct((half, toks), dtype),
        cost_estimate=pl.CostEstimate(
            flops=4 * half * columns * toks,
            bytes_accessed=4 * half * columns + 4 * half * toks,
            transcendentals=0,
        ),
        compiler_params=pltpu.CompilerParams(vmem_limit_bytes=vmem_bytes),
    )(lm_a, lm_b, rows_a, rows_b)


def vocab_logits(hidden, lm_a, lm_b):
    half, columns = lm_a.shape
    toks = hidden.shape[1]
    step = half // 2
    lanes = 128

    def kernel(h_ref, a_ref, b_ref, out_ref, coded_ref):
        part_a = dot(h_ref[...], a_ref[...], ((0,), (0,)))
        part_b = dot(h_ref[...], b_ref[...], ((0,), (0,)))

        @pl.when(pl.program_id(0) == 0)
        def _():
            out_ref[:, :columns] = part_a
            out_ref[:, columns:] = part_b

        @pl.when(pl.program_id(0) > 0)
        def _():
            value = out_ref[...] + jnp.concatenate([part_a, part_b], 1)
            out_ref[...] = value
            size = jnp.max(jnp.abs(value), axis=1, keepdims=True)
            power = jnp.ceil(jnp.log(jnp.maximum(size, 1e-30)) * (1.0 / ln2))
            code = jnp.floor(value * (int16_top * jnp.exp(power * -ln2)) + 0.5)
            code = jnp.clip(code, -int16_top, int16_top)
            coded_ref[:, : 2 * columns] = code.astype(jnp.int32).astype(jnp.int16)
            power = jnp.broadcast_to(power, (toks, lanes))
            coded_ref[:, 2 * columns :] = power.astype(jnp.int32).astype(jnp.int16)

    weights = pl.BlockSpec((step, columns), lambda i: (i, 0))
    return pl.pallas_call(
        kernel,
        grid=(half // step,),
        in_specs=[pl.BlockSpec((step, toks), lambda i: (i, 0)), weights, weights],
        out_specs=[
            pl.BlockSpec((toks, 2 * columns), lambda i: (0, 0)),
            pl.BlockSpec((toks, 2 * columns + lanes), lambda i: (0, 0)),
        ],
        out_shape=[
            jax.ShapeDtypeStruct((toks, 2 * columns), f32),
            jax.ShapeDtypeStruct((toks, 2 * columns + lanes), jnp.int16),
        ],
        cost_estimate=pl.CostEstimate(
            flops=4 * half * columns * toks,
            bytes_accessed=4 * half * columns + 2 * half * toks,
            transcendentals=0,
        ),
        compiler_params=pltpu.CompilerParams(vmem_limit_bytes=vmem_bytes),
    )(hidden, lm_a, lm_b)


def combine(stats, own, product, target_cols):
    half, toks = product.shape
    step = half

    def kernel(stats_ref, own_ref, product_ref, target_ref, out_ref, ratio_ref):
        tops, rests, targets = stats_ref[:, 0, :], stats_ref[:, 1, :], stats_ref[:, 2, :]
        top, scale = own_ref[0:1, :], own_ref[1:2, :]
        all_top = jnp.max(tops, axis=0, keepdims=True)
        weight = jnp.exp(tops - all_top)
        rest = jnp.sum(rests * weight, axis=0, keepdims=True)
        total = rest + jnp.sum(targets * weight, axis=0, keepdims=True)
        ratio = scale * jnp.exp(top - all_top) / total
        ratio_ref[...] = ratio
        value = product_ref[...].astype(f32) * ratio - target_ref[...].astype(f32) * (scale * rest / total)
        out_ref[...] = value.astype(out_ref.dtype)

    rows = pl.BlockSpec((step, toks), lambda i: (i, 0))
    return pl.pallas_call(
        kernel,
        grid=(half // step,),
        in_specs=[
            pl.BlockSpec(stats.shape, lambda i: (0, 0, 0)),
            pl.BlockSpec(own.shape, lambda i: (0, 0)),
            rows,
            rows,
        ],
        out_specs=[rows, pl.BlockSpec((1, toks), lambda i: (0, 0))],
        out_shape=[
            jax.ShapeDtypeStruct((half, toks), bf16),
            jax.ShapeDtypeStruct((1, toks), f32),
        ],
        cost_estimate=pl.CostEstimate(
            flops=4 * half * toks, bytes_accessed=8 * half * toks, transcendentals=0
        ),
        compiler_params=pltpu.CompilerParams(vmem_limit_bytes=vmem_bytes),
    )(stats, own, product, target_cols)


def on_device(trunk_rows, res_weight, res_bias, lm_weight, next_ids, valid_mask):
    head = lax.axis_index("x")
    ylo, z, core, yhi = (lax.axis_index(a) for a in ("ylo", "z", "core", "yhi"))
    n_x = lax.axis_size("x")
    n_plane = lax.axis_size("ylo") * lax.axis_size("z")
    n_all = n_plane * lax.axis_size("yhi")
    rows, width = trunk_rows.shape
    toks = n_all * rows

    res_own = res_weight[0].T
    cols = res_own.shape[0]
    pair = 2 * cols
    lm_own = lm_weight[0]
    half, vocab_width = lm_own.shape
    res_other = swap(res_own, "core")
    lm_other = swap(lm_own, "core")
    first = core == 0
    res_pair = jnp.concatenate(
        [jnp.where(first, res_own, res_other), jnp.where(first, res_other, res_own)], 0
    )
    bias_own = res_bias[0].astype(f32)
    bias_other = swap(bias_own, "core")
    bias_pair = jnp.concatenate(
        [jnp.where(first, bias_own, bias_other), jnp.where(first, bias_other, bias_own)]
    )

    chip = ylo * lax.axis_size("z") + z
    block = yhi * n_plane + chip
    odd = head % 2
    half_cols = width // 2
    quarter = half_cols // 2
    iota_r = lax.broadcasted_iota(jnp.int32, (pair, half_cols), 0)
    iota_c = lax.broadcasted_iota(jnp.int32, (pair, half_cols), 1)

    select = jnp.concatenate(
        [(iota_r + block * pair == iota_c + side * half_cols).astype(bf16) for side in (0, 1)], 1
    )
    res_aug = jnp.concatenate([res_pair, select], 0)
    near = lax.dynamic_slice_in_dim(res_aug, odd * half_cols, half_cols, 1)
    far = lax.dynamic_slice_in_dim(res_aug, (1 - odd) * half_cols, half_cols, 1)

    def shift(value, step):
        return lax.ppermute(value, "x", [(i, (i + step) % n_x) for i in range(n_x)])

    line = ("ylo", "yhi")
    n_z = lax.axis_size("z")
    n_y = lax.axis_size("ylo") * lax.axis_size("yhi")
    y = yhi * lax.axis_size("ylo") + ylo

    def z_shift(value, step):
        return lax.ppermute(value, "z", [(i, (i + step) % n_z) for i in range(n_z)])

    def line_index(at):
        return at % 2 * 2 + at // 2

    def y_flip(value, flip):
        pairs = [(line_index(i), line_index(i ^ flip)) for i in range(n_y)]
        return lax.ppermute(value, line, pairs)

    def place(buffer, block, at, row=0):
        return lax.dynamic_update_slice(buffer, block[None], (at, row, 0))

    seen = exchange(jnp.broadcast_to(trunk_rows[None], (n_y, rows, width)), line)
    seen = seen.reshape(n_y * rows, width)
    cut = n_y * rows // 2
    up = down = seen
    trunk = place(jnp.zeros((n_z, n_y * rows, width), bf16), seen, z)
    for step in range(1, n_z // 2):
        up, down = z_shift(up, 1), z_shift(down, -1)
        if step == n_z // 2 - 1:
            up, down, res_aug = lax.optimization_barrier((up, down, res_aug))
        trunk = place(trunk, up, (z - step) % n_z)
        trunk = place(trunk, down, (z + step) % n_z)
    up, down = z_shift(up[:cut], 1), z_shift(down[cut:], -1)
    trunk = place(trunk, up, (z + n_z // 2) % n_z)
    trunk = place(trunk, down, (z + n_z // 2) % n_z, cut)
    trunk = trunk.reshape(toks, width)

    def own_tokens(values):
        values = lax.dynamic_slice_in_dim(values, head + 1, 2 * toks)
        values = values.reshape(lax.axis_size("ylo"), n_z, 2, lax.axis_size("yhi"), rows)
        values = lax.dynamic_index_in_dim(values, core, 2, keepdims=False)
        return values.transpose(1, 0, 2, 3).reshape(toks)

    tok_ids = own_tokens(next_ids)
    live = own_tokens(valid_mask).astype(f32)
    scale = loss_scale * jnp.power(jnp.float32(0.8), head.astype(f32)) * live
    lanes = lax.broadcasted_iota(jnp.int32, (1, vocab_width), 1)

    def onehot(owner):
        return (tok_ids - (chip * 2 + owner) * vocab_width)[:, None] == lanes

    hot_own, hot_other = onehot(core), onehot(1 - core)
    target_cols = vocab_product(
        lm_own, lm_other, hot_own.astype(bf16), hot_other.astype(bf16), bf16
    )
    both = dot(res_aug, trunk, ((1,), (1,)))
    pre = both[:pair] + bias_pair[:, None]
    hidden = (both[pair:] + jax.nn.silu(pre)).astype(bf16)
    hidden_half = exchange(
        jnp.broadcast_to(hidden[None], (n_plane, pair, toks)), plane
    ).reshape(half, toks)
    target_cols, hidden_half = lax.optimization_barrier((target_cols, hidden_half))

    logits, coded = vocab_logits(hidden_half, lm_own, lm_other)
    coded = swap(coded, "yhi").astype(f32)
    logits = logits + coded[:, : 2 * vocab_width] * (
        jnp.exp(coded[:, 2 * vocab_width : 2 * vocab_width + 1] * ln2) * (1.0 / int16_top)
    )
    logits_own, logits_other = logits[:, :vocab_width], logits[:, vocab_width:]
    top = jnp.maximum(jnp.max(logits_own, axis=1), jnp.max(logits_other, axis=1))
    exp_own = jnp.exp(logits_own - top[:, None])
    exp_other = jnp.exp(logits_other - top[:, None])
    rest_own = jnp.where(hot_own, 0.0, exp_own)
    rest_other = jnp.where(hot_other, 0.0, exp_other)
    rest = jnp.sum(rest_own, axis=1) + jnp.sum(rest_other, axis=1)
    at_target = jnp.sum(jnp.where(hot_own, exp_own, 0.0), axis=1) + jnp.sum(
        jnp.where(hot_other, exp_other, 0.0), axis=1
    )
    stats = jnp.stack([top, rest, at_target])
    stats = exchange(jnp.broadcast_to(stats[None], (n_plane, 3, toks)), plane)
    part_grad = vocab_product(
        lm_own, lm_other, rest_own.astype(bf16), rest_other.astype(bf16), bf16
    )
    part_grad, ratio = combine(stats, jnp.stack([top, scale]), part_grad, target_cols)
    ratio = ratio[0]
    parts = exchange(part_grad.reshape(n_plane, pair, toks), plane)
    hidden_grad = jnp.sum(parts.astype(f32), axis=0)
    pre_grad = hidden_grad * silu_grad(pre)
    pre_round = pre_grad.astype(bf16)

    def grad_of(exps, hot):
        return jnp.where(hot, ratio[:, None] * exps - scale[:, None], ratio[:, None] * exps).astype(
            bf16
        )

    grad_own = grad_of(exp_own, hot_own)
    grad_other = grad_of(exp_other, hot_other)
    hidden_both = jnp.concatenate([hidden_half, swap(hidden_half, "core")], 1)
    grad_both = jnp.concatenate([grad_own, swap(grad_other, "core")], 0)
    lm_grad = dot(hidden_both, grad_both, ((1,), (0,))).astype(bf16)
    pre_own = lax.dynamic_slice_in_dim(pre_grad, core * cols, cols, 0)
    pre_sibling = swap(lax.dynamic_slice_in_dim(pre_grad, (1 - core) * cols, cols, 0), "core")
    bias_grad = jnp.sum(pre_own, axis=1) + jnp.sum(pre_sibling, axis=1)
    pre_both = jnp.concatenate([pre_own, pre_sibling], 1).astype(bf16)

    trunk_both = jnp.concatenate([trunk, swap(trunk, "core")], 0)
    res_grad = dot(pre_both, trunk_both, ((1,), (0,))).astype(bf16)
    order = lax.broadcasted_iota(jnp.int32, (toks, toks), 1)
    order_y, order_z = order // (rows * n_z), order // rows % n_z
    order = (order_z * n_y + line_index(order_y)) * rows + order % rows
    order = (order == lax.broadcasted_iota(jnp.int32, (toks, toks), 0)).astype(bf16)
    both_grad = jnp.concatenate([pre_round, hidden_grad.astype(bf16)], 0)
    both_grad = dot(both_grad, order, ((1,), (0,))).astype(bf16)
    given = dot(both_grad, far, ((0,), (0,))).astype(bf16)
    got_left = shift(given[:, quarter:], 1)
    got_right = shift(given[:, :quarter], -1)
    keep = dot(both_grad, near, ((0,), (0,)))
    by_x = jnp.concatenate(
        [keep[:, :quarter] + got_right.astype(f32), keep[:, quarter:] + got_left.astype(f32)], 1
    ).astype(bf16)
    by_x = by_x.reshape(n_y, n_z * rows, half_cols)
    by_y = lax.dynamic_index_in_dim(by_x, y, 0, keepdims=False).astype(f32)
    for flip in (1, 3, 2):
        sent = lax.dynamic_index_in_dim(by_x, y ^ flip, 0, keepdims=False)
        pairs = [(line_index(i), line_index(i ^ flip)) for i in range(n_y)]
        got = lax.ppermute(sent, line, pairs)
        by_y = by_y + got.astype(f32)
    by_z = exchange(by_y.astype(bf16).reshape(n_z, rows, half_cols), "z")
    by_z, res_grad = lax.optimization_barrier((by_z, res_grad))
    summed = jnp.sum(by_z.astype(f32), axis=0)
    here = summed + shift(summed, 2)
    there = shift(summed, 1) + shift(summed, -1)
    trunk_grad = jnp.concatenate(
        [jnp.where(odd == 0, here, there), jnp.where(odd == 0, there, here)], 1
    )

    return (trunk_grad, res_grad.T[None], bias_grad[None], lm_grad[None])


def solution(mesh):
    fine = Mesh(mesh.devices.reshape(4, 2, 8, 2, 2), ("x", "ylo", "z", "core", "yhi"))
    vocab = ("ylo", "z", "core")
    in_specs = (
        P((*vocab, "yhi"), None),
        P("x", None, ("yhi", *vocab)),
        P("x", ("yhi", *vocab)),
        P("x", "yhi", vocab),
        P(),
        P(),
    )
    out_specs = (
        P((*vocab, "yhi"), None),
        P("x", None, ("yhi", *vocab)),
        P("x", ("yhi", *vocab)),
        P("x", "yhi", vocab),
    )
    return jax.shard_map(
        on_device, mesh=fine, in_specs=in_specs, out_specs=out_specs, check_vma=False
    )
```

```python
import jax
import jax.numpy as jnp
from jax import lax
from jax.experimental import pallas as pl
from jax.experimental.pallas import tpu as pltpu
from jax.sharding import Mesh
from jax.sharding import PartitionSpec as P

loss_scale = 16.0
int16_top = 32767.0
ln2 = 0.6931471805599453
vmem_bytes = 60 * 2**20
f32 = jnp.float32
bf16 = jnp.bfloat16
plane = ("ylo", "z")
plane_all = ("ylo", "z", "yhi")


def silu_grad(value):
    sigma = jax.nn.sigmoid(value)
    return sigma * (1.0 + value * (1.0 - sigma))


def swap(value, axis):
    return lax.ppermute(value, axis, [(0, 1), (1, 0)])


def exchange(value, axes):
    return lax.all_to_all(value, axes, 0, 0, tiled=True)


def dot(a, b, contract):
    return lax.dot_general(a, b, ((contract[0], contract[1]), ((), ())), preferred_element_type=f32)


def vocab_product(lm_a, lm_b, rows_a, rows_b, dtype):
    half, columns = lm_a.shape
    toks = rows_a.shape[0]
    step = half // 2

    def kernel(a_ref, b_ref, ra_ref, rb_ref, out_ref):
        total = dot(a_ref[...], ra_ref[...], ((1,), (1,)))
        total = total + dot(b_ref[...], rb_ref[...], ((1,), (1,)))
        out_ref[...] = total.astype(out_ref.dtype)

    weights = pl.BlockSpec((step, columns), lambda i: (i, 0))
    whole = pl.BlockSpec((toks, columns), lambda i: (0, 0))
    return pl.pallas_call(
        kernel,
        grid=(half // step,),
        in_specs=[weights, weights, whole, whole],
        out_specs=pl.BlockSpec((step, toks), lambda i: (i, 0)),
        out_shape=jax.ShapeDtypeStruct((half, toks), dtype),
        cost_estimate=pl.CostEstimate(
            flops=4 * half * columns * toks,
            bytes_accessed=4 * half * columns + 4 * half * toks,
            transcendentals=0,
        ),
        compiler_params=pltpu.CompilerParams(vmem_limit_bytes=vmem_bytes),
    )(lm_a, lm_b, rows_a, rows_b)


def vocab_logits(hidden, lm_a, lm_b):
    half, columns = lm_a.shape
    toks = hidden.shape[1]
    step = half // 2
    lanes = 128

    def kernel(h_ref, a_ref, b_ref, out_ref, coded_ref):
        part_a = dot(h_ref[...], a_ref[...], ((0,), (0,)))
        part_b = dot(h_ref[...], b_ref[...], ((0,), (0,)))

        @pl.when(pl.program_id(0) == 0)
        def _():
            out_ref[:, :columns] = part_a
            out_ref[:, columns:] = part_b

        @pl.when(pl.program_id(0) > 0)
        def _():
            value = out_ref[...] + jnp.concatenate([part_a, part_b], 1)
            out_ref[...] = value
            size = jnp.max(jnp.abs(value), axis=1, keepdims=True)
            power = jnp.ceil(jnp.log(jnp.maximum(size, 1e-30)) * (1.0 / ln2))
            code = jnp.floor(value * (int16_top * jnp.exp(power * -ln2)) + 0.5)
            code = jnp.clip(code, -int16_top, int16_top)
            coded_ref[:, : 2 * columns] = code.astype(jnp.int32).astype(jnp.int16)
            power = jnp.broadcast_to(power, (toks, lanes))
            coded_ref[:, 2 * columns :] = power.astype(jnp.int32).astype(jnp.int16)

    weights = pl.BlockSpec((step, columns), lambda i: (i, 0))
    return pl.pallas_call(
        kernel,
        grid=(half // step,),
        in_specs=[pl.BlockSpec((step, toks), lambda i: (i, 0)), weights, weights],
        out_specs=[
            pl.BlockSpec((toks, 2 * columns), lambda i: (0, 0)),
            pl.BlockSpec((toks, 2 * columns + lanes), lambda i: (0, 0)),
        ],
        out_shape=[
            jax.ShapeDtypeStruct((toks, 2 * columns), f32),
            jax.ShapeDtypeStruct((toks, 2 * columns + lanes), jnp.int16),
        ],
        cost_estimate=pl.CostEstimate(
            flops=4 * half * columns * toks,
            bytes_accessed=4 * half * columns + 2 * half * toks,
            transcendentals=0,
        ),
        compiler_params=pltpu.CompilerParams(vmem_limit_bytes=vmem_bytes),
    )(hidden, lm_a, lm_b)


def combine(stats, own, product, target_cols):
    half, toks = product.shape
    step = half

    def kernel(stats_ref, own_ref, product_ref, target_ref, out_ref, ratio_ref):
        tops, rests, targets = stats_ref[:, 0, :], stats_ref[:, 1, :], stats_ref[:, 2, :]
        top, scale = own_ref[0:1, :], own_ref[1:2, :]
        all_top = jnp.max(tops, axis=0, keepdims=True)
        weight = jnp.exp(tops - all_top)
        rest = jnp.sum(rests * weight, axis=0, keepdims=True)
        total = rest + jnp.sum(targets * weight, axis=0, keepdims=True)
        ratio = scale * jnp.exp(top - all_top) / total
        ratio_ref[...] = ratio
        value = product_ref[...].astype(f32) * ratio - target_ref[...].astype(f32) * (scale * rest / total)
        out_ref[...] = value.astype(out_ref.dtype)

    rows = pl.BlockSpec((step, toks), lambda i: (i, 0))
    return pl.pallas_call(
        kernel,
        grid=(half // step,),
        in_specs=[
            pl.BlockSpec(stats.shape, lambda i: (0, 0, 0)),
            pl.BlockSpec(own.shape, lambda i: (0, 0)),
            rows,
            rows,
        ],
        out_specs=[rows, pl.BlockSpec((1, toks), lambda i: (0, 0))],
        out_shape=[
            jax.ShapeDtypeStruct((half, toks), bf16),
            jax.ShapeDtypeStruct((1, toks), f32),
        ],
        cost_estimate=pl.CostEstimate(
            flops=4 * half * toks, bytes_accessed=8 * half * toks, transcendentals=0
        ),
        compiler_params=pltpu.CompilerParams(vmem_limit_bytes=16 * 2**20),
    )(stats, own, product, target_cols)


def on_device(trunk_rows, res_weight, res_bias, lm_weight, next_ids, valid_mask):
    head = lax.axis_index("x")
    ylo, z, core, yhi = (lax.axis_index(a) for a in ("ylo", "z", "core", "yhi"))
    n_x = lax.axis_size("x")
    n_plane = lax.axis_size("ylo") * lax.axis_size("z")
    n_all = n_plane * lax.axis_size("yhi")
    rows, width = trunk_rows.shape
    toks = n_all * rows

    res_own = res_weight[0].T
    cols = res_own.shape[0]
    pair = 2 * cols
    lm_own = lm_weight[0]
    half, vocab_width = lm_own.shape
    res_other = swap(res_own, "core")
    lm_other = swap(lm_own, "core")
    first = core == 0
    res_pair = jnp.concatenate(
        [jnp.where(first, res_own, res_other), jnp.where(first, res_other, res_own)], 0
    )
    bias_own = res_bias[0].astype(f32)
    bias_other = swap(bias_own, "core")
    bias_pair = jnp.concatenate(
        [jnp.where(first, bias_own, bias_other), jnp.where(first, bias_other, bias_own)]
    )

    chip = ylo * lax.axis_size("z") + z
    block = yhi * n_plane + chip
    odd = head % 2
    half_cols = width // 2
    quarter = half_cols // 2
    iota_r = lax.broadcasted_iota(jnp.int32, (pair, half_cols), 0)
    iota_c = lax.broadcasted_iota(jnp.int32, (pair, half_cols), 1)

    select = jnp.concatenate(
        [(iota_r + block * pair == iota_c + side * half_cols).astype(bf16) for side in (0, 1)], 1
    )
    res_aug = jnp.concatenate([res_pair, select], 0)
    near = lax.dynamic_slice_in_dim(res_aug, odd * half_cols, half_cols, 1)
    far = lax.dynamic_slice_in_dim(res_aug, (1 - odd) * half_cols, half_cols, 1)

    def shift(value, step):
        return lax.ppermute(value, "x", [(i, (i + step) % n_x) for i in range(n_x)])

    line = ("ylo", "yhi")
    n_z = lax.axis_size("z")
    n_y = lax.axis_size("ylo") * lax.axis_size("yhi")
    y = yhi * lax.axis_size("ylo") + ylo

    def z_shift(value, step):
        return lax.ppermute(value, "z", [(i, (i + step) % n_z) for i in range(n_z)])

    def line_index(at):
        return at % 2 * 2 + at // 2

    def y_flip(value, flip):
        pairs = [(line_index(i), line_index(i ^ flip)) for i in range(n_y)]
        return lax.ppermute(value, line, pairs)

    def place(buffer, block, at, row=0):
        return lax.dynamic_update_slice(buffer, block[None], (at, row, 0))

    seen = exchange(jnp.broadcast_to(trunk_rows[None], (n_y, rows, width)), line)
    seen = seen.reshape(n_y * rows, width)
    cut = n_y * rows // 2
    up = down = seen
    trunk = place(jnp.zeros((n_z, n_y * rows, width), bf16), seen, z)
    for step in range(1, n_z // 2):
        up, down = z_shift(up, 1), z_shift(down, -1)
        if step == n_z // 2 - 1:
            up, down, res_aug = lax.optimization_barrier((up, down, res_aug))
        trunk = place(trunk, up, (z - step) % n_z)
        trunk = place(trunk, down, (z + step) % n_z)
    up, down = z_shift(up[:cut], 1), z_shift(down[cut:], -1)
    trunk = place(trunk, up, (z + n_z // 2) % n_z)
    trunk = place(trunk, down, (z + n_z // 2) % n_z, cut)
    trunk = trunk.reshape(toks, width)

    def own_tokens(values):
        values = lax.dynamic_slice_in_dim(values, head + 1, 2 * toks)
        values = values.reshape(lax.axis_size("ylo"), n_z, 2, lax.axis_size("yhi"), rows)
        values = lax.dynamic_index_in_dim(values, core, 2, keepdims=False)
        return values.transpose(1, 0, 2, 3).reshape(toks)

    tok_ids = own_tokens(next_ids)
    live = own_tokens(valid_mask).astype(f32)
    scale = loss_scale * jnp.power(jnp.float32(0.8), head.astype(f32)) * live
    lanes = lax.broadcasted_iota(jnp.int32, (1, vocab_width), 1)

    def onehot(owner):
        return (tok_ids - (chip * 2 + owner) * vocab_width)[:, None] == lanes

    hot_own, hot_other = onehot(core), onehot(1 - core)
    target_cols = vocab_product(
        lm_own, lm_other, hot_own.astype(bf16), hot_other.astype(bf16), bf16
    )
    both = dot(res_aug, trunk, ((1,), (1,)))
    pre = both[:pair] + bias_pair[:, None]
    hidden = (both[pair:] + jax.nn.silu(pre)).astype(bf16)
    hidden_half = exchange(
        jnp.broadcast_to(hidden[None], (n_plane, pair, toks)), plane
    ).reshape(half, toks)
    target_cols, hidden_half = lax.optimization_barrier((target_cols, hidden_half))

    logits, coded = vocab_logits(hidden_half, lm_own, lm_other)
    coded = swap(coded, "yhi").astype(f32)
    logits = logits + coded[:, : 2 * vocab_width] * (
        jnp.exp(coded[:, 2 * vocab_width : 2 * vocab_width + 1] * ln2) * (1.0 / int16_top)
    )
    logits_own, logits_other = logits[:, :vocab_width], logits[:, vocab_width:]
    top = jnp.maximum(jnp.max(logits_own, axis=1), jnp.max(logits_other, axis=1))
    exp_own = jnp.exp(logits_own - top[:, None])
    exp_other = jnp.exp(logits_other - top[:, None])
    rest_own = jnp.where(hot_own, 0.0, exp_own)
    rest_other = jnp.where(hot_other, 0.0, exp_other)
    rest = jnp.sum(rest_own, axis=1) + jnp.sum(rest_other, axis=1)
    at_target = jnp.sum(jnp.where(hot_own, exp_own, 0.0), axis=1) + jnp.sum(
        jnp.where(hot_other, exp_other, 0.0), axis=1
    )
    stats = jnp.stack([top, rest, at_target])
    stats = exchange(jnp.broadcast_to(stats[None], (n_plane, 3, toks)), plane)
    part_grad = vocab_product(
        lm_own, lm_other, rest_own.astype(bf16), rest_other.astype(bf16), bf16
    )
    part_grad, ratio = combine(stats, jnp.stack([top, scale]), part_grad, target_cols)
    ratio = ratio[0]
    parts = exchange(part_grad.reshape(n_plane, pair, toks), plane)
    hidden_grad = jnp.sum(parts.astype(f32), axis=0)
    pre_grad = hidden_grad * silu_grad(pre)
    pre_round = pre_grad.astype(bf16)

    def grad_of(exps, hot):
        return jnp.where(hot, ratio[:, None] * exps - scale[:, None], ratio[:, None] * exps).astype(
            bf16
        )

    grad_own = grad_of(exp_own, hot_own)
    grad_other = grad_of(exp_other, hot_other)
    hidden_both = jnp.concatenate([hidden_half, swap(hidden_half, "core")], 1)
    grad_both = jnp.concatenate([grad_own, swap(grad_other, "core")], 0)
    lm_grad = dot(hidden_both, grad_both, ((1,), (0,))).astype(bf16)
    pre_own = lax.dynamic_slice_in_dim(pre_grad, core * cols, cols, 0)
    pre_sibling = swap(lax.dynamic_slice_in_dim(pre_grad, (1 - core) * cols, cols, 0), "core")
    bias_grad = jnp.sum(pre_own, axis=1) + jnp.sum(pre_sibling, axis=1)
    pre_both = jnp.concatenate([pre_own, pre_sibling], 1).astype(bf16)

    trunk_both = jnp.concatenate([trunk, swap(trunk, "core")], 0)
    res_grad = dot(pre_both, trunk_both, ((1,), (0,))).astype(bf16)
    order = lax.broadcasted_iota(jnp.int32, (toks, toks), 1)
    order_y, order_z = order // (rows * n_z), order // rows % n_z
    order = (order_z * n_y + line_index(order_y)) * rows + order % rows
    order = (order == lax.broadcasted_iota(jnp.int32, (toks, toks), 0)).astype(bf16)
    both_grad = jnp.concatenate([pre_round, hidden_grad.astype(bf16)], 0)
    both_grad = dot(both_grad, order, ((1,), (0,))).astype(bf16)
    given = dot(both_grad, far, ((0,), (0,))).astype(bf16)
    got_left = shift(given[:, quarter:], 1)
    got_right = shift(given[:, :quarter], -1)
    keep = dot(both_grad, near, ((0,), (0,)))
    by_x = jnp.concatenate(
        [keep[:, :quarter] + got_right.astype(f32), keep[:, quarter:] + got_left.astype(f32)], 1
    ).astype(bf16)
    by_x = by_x.reshape(n_y, n_z * rows, half_cols)
    by_y = lax.dynamic_index_in_dim(by_x, y, 0, keepdims=False).astype(f32)
    for flip in (1, 3, 2):
        sent = lax.dynamic_index_in_dim(by_x, y ^ flip, 0, keepdims=False)
        pairs = [(line_index(i), line_index(i ^ flip)) for i in range(n_y)]
        got = lax.ppermute(sent, line, pairs)
        by_y = by_y + got.astype(f32)
    by_z = exchange(by_y.astype(bf16).reshape(n_z, rows, half_cols), "z")
    by_z, res_grad = lax.optimization_barrier((by_z, res_grad))
    summed = jnp.sum(by_z.astype(f32), axis=0)
    here = summed + shift(summed, 2)
    there = shift(summed, 1) + shift(summed, -1)
    trunk_grad = jnp.concatenate(
        [jnp.where(odd == 0, here, there), jnp.where(odd == 0, there, here)], 1
    )

    return (trunk_grad, res_grad.T[None], bias_grad[None], lm_grad[None])


def solution(mesh):
    fine = Mesh(mesh.devices.reshape(4, 2, 8, 2, 2), ("x", "ylo", "z", "core", "yhi"))
    vocab = ("ylo", "z", "core")
    in_specs = (
        P((*vocab, "yhi"), None),
        P("x", None, ("yhi", *vocab)),
        P("x", ("yhi", *vocab)),
        P("x", "yhi", vocab),
        P(),
        P(),
    )
    out_specs = (
        P((*vocab, "yhi"), None),
        P("x", None, ("yhi", *vocab)),
        P("x", ("yhi", *vocab)),
        P("x", "yhi", vocab),
    )
    return jax.shard_map(
        on_device, mesh=fine, in_specs=in_specs, out_specs=out_specs, check_vma=False
    )
```

```python
import jax
import jax.numpy as jnp
from jax import lax
from jax.experimental import pallas as pl
from jax.experimental.pallas import tpu as pltpu
from jax.sharding import Mesh
from jax.sharding import PartitionSpec as P

loss_scale = 16.0
int16_top = 32767.0
ln2 = 0.6931471805599453
vmem_bytes = 60 * 2**20
f32 = jnp.float32
bf16 = jnp.bfloat16
plane = ("ylo", "z")
plane_all = ("ylo", "z", "yhi")


def silu_grad(value):
    sigma = jax.nn.sigmoid(value)
    return sigma * (1.0 + value * (1.0 - sigma))


def swap(value, axis):
    return lax.ppermute(value, axis, [(0, 1), (1, 0)])


def exchange(value, axes):
    return lax.all_to_all(value, axes, 0, 0, tiled=True)


def dot(a, b, contract):
    return lax.dot_general(a, b, ((contract[0], contract[1]), ((), ())), preferred_element_type=f32)


def vocab_product(lm_a, lm_b, rows_a, rows_b, dtype):
    half, columns = lm_a.shape
    toks = rows_a.shape[0]
    step = half // 2

    def kernel(a_ref, b_ref, ra_ref, rb_ref, out_ref):
        total = dot(a_ref[...], ra_ref[...], ((1,), (1,)))
        total = total + dot(b_ref[...], rb_ref[...], ((1,), (1,)))
        out_ref[...] = total.astype(out_ref.dtype)

    weights = pl.BlockSpec((step, columns), lambda i: (i, 0))
    whole = pl.BlockSpec((toks, columns), lambda i: (0, 0))
    return pl.pallas_call(
        kernel,
        grid=(half // step,),
        in_specs=[weights, weights, whole, whole],
        out_specs=pl.BlockSpec((step, toks), lambda i: (i, 0)),
        out_shape=jax.ShapeDtypeStruct((half, toks), dtype),
        cost_estimate=pl.CostEstimate(
            flops=4 * half * columns * toks,
            bytes_accessed=4 * half * columns + 4 * half * toks,
            transcendentals=0,
        ),
        compiler_params=pltpu.CompilerParams(vmem_limit_bytes=vmem_bytes),
    )(lm_a, lm_b, rows_a, rows_b)


def vocab_logits(hidden, lm_a, lm_b):
    half, columns = lm_a.shape
    toks = hidden.shape[1]
    step = half // 2
    lanes = 128

    def kernel(h_ref, a_ref, b_ref, out_ref, coded_ref):
        part_a = dot(h_ref[...], a_ref[...], ((0,), (0,)))
        part_b = dot(h_ref[...], b_ref[...], ((0,), (0,)))

        @pl.when(pl.program_id(0) == 0)
        def _():
            out_ref[:, :columns] = part_a
            out_ref[:, columns:] = part_b

        @pl.when(pl.program_id(0) > 0)
        def _():
            value = out_ref[...] + jnp.concatenate([part_a, part_b], 1)
            out_ref[...] = value
            size = jnp.max(jnp.abs(value), axis=1, keepdims=True)
            power = jnp.ceil(jnp.log(jnp.maximum(size, 1e-30)) * (1.0 / ln2))
            code = jnp.floor(value * (int16_top * jnp.exp(power * -ln2)) + 0.5)
            code = jnp.clip(code, -int16_top, int16_top)
            coded_ref[:, : 2 * columns] = code.astype(jnp.int32).astype(jnp.int16)
            power = jnp.broadcast_to(power, (toks, lanes))
            coded_ref[:, 2 * columns :] = power.astype(jnp.int32).astype(jnp.int16)

    weights = pl.BlockSpec((step, columns), lambda i: (i, 0))
    return pl.pallas_call(
        kernel,
        grid=(half // step,),
        in_specs=[pl.BlockSpec((step, toks), lambda i: (i, 0)), weights, weights],
        out_specs=[
            pl.BlockSpec((toks, 2 * columns), lambda i: (0, 0)),
            pl.BlockSpec((toks, 2 * columns + lanes), lambda i: (0, 0)),
        ],
        out_shape=[
            jax.ShapeDtypeStruct((toks, 2 * columns), f32),
            jax.ShapeDtypeStruct((toks, 2 * columns + lanes), jnp.int16),
        ],
        cost_estimate=pl.CostEstimate(
            flops=4 * half * columns * toks,
            bytes_accessed=4 * half * columns + 2 * half * toks,
            transcendentals=0,
        ),
        compiler_params=pltpu.CompilerParams(vmem_limit_bytes=vmem_bytes),
    )(hidden, lm_a, lm_b)


def local_softmax(logits, coded, spots, copies):
    toks, columns = logits.shape
    width = columns // 2

    def kernel(logits_ref, coded_ref, spots_ref, total_ref, rest_a_ref, rest_b_ref, stats_ref):
        power = coded_ref[:, columns : columns + 1].astype(jnp.int32).astype(f32)
        code = coded_ref[:, :columns].astype(jnp.int32).astype(f32)
        total = logits_ref[...] + code * (jnp.exp(power * ln2) * (1.0 / int16_top))
        total_ref[...] = total
        top = jnp.max(total, axis=1, keepdims=True)
        rests, targets = 0.0, 0.0
        for side, out_ref in ((0, rest_a_ref), (1, rest_b_ref)):
            exps = jnp.exp(total[:, side * width : (side + 1) * width] - top)
            lanes = lax.broadcasted_iota(jnp.int32, (toks, width), 1)
            hot = lanes == spots_ref[:, side : side + 1]
            rest = jnp.where(hot, 0.0, exps)
            out_ref[...] = rest.astype(bf16)
            rests = rests + jnp.sum(rest, axis=1, keepdims=True)
            targets = targets + jnp.sum(jnp.where(hot, exps, 0.0), axis=1, keepdims=True)
        for row, value in enumerate((top, rests, targets)):
            line = jnp.broadcast_to(value, (toks, toks)).T[0:1]
            stats_ref[:, row, :] = jnp.broadcast_to(line, (copies, toks))

    return pl.pallas_call(
        kernel,
        out_shape=[
            jax.ShapeDtypeStruct((toks, columns), f32),
            jax.ShapeDtypeStruct((toks, width), bf16),
            jax.ShapeDtypeStruct((toks, width), bf16),
            jax.ShapeDtypeStruct((copies, 3, toks), f32),
        ],
        cost_estimate=pl.CostEstimate(
            flops=12 * toks * columns,
            bytes_accessed=12 * toks * columns,
            transcendentals=toks * columns,
        ),
        compiler_params=pltpu.CompilerParams(vmem_limit_bytes=vmem_bytes),
    )(logits, coded, spots)


def combine(stats, own, scale, product, target_cols):
    half, toks = product.shape
    step = half

    def kernel(stats_ref, own_ref, scale_ref, product_ref, target_ref, out_ref, ratio_ref):
        tops, rests, targets = stats_ref[:, 0, :], stats_ref[:, 1, :], stats_ref[:, 2, :]
        top, scale = own_ref[0:1, 0, :], scale_ref[...]
        all_top = jnp.max(tops, axis=0, keepdims=True)
        weight = jnp.exp(tops - all_top)
        rest = jnp.sum(rests * weight, axis=0, keepdims=True)
        total = rest + jnp.sum(targets * weight, axis=0, keepdims=True)
        ratio = scale * jnp.exp(top - all_top) / total
        ratio_ref[...] = ratio
        value = product_ref[...].astype(f32) * ratio - target_ref[...].astype(f32) * (scale * rest / total)
        out_ref[...] = value.astype(out_ref.dtype)

    rows = pl.BlockSpec((step, toks), lambda i: (i, 0))
    return pl.pallas_call(
        kernel,
        grid=(half // step,),
        in_specs=[
            pl.BlockSpec(stats.shape, lambda i: (0, 0, 0)),
            pl.BlockSpec(own.shape, lambda i: (0, 0, 0)),
            pl.BlockSpec(scale.shape, lambda i: (0, 0)),
            rows,
            rows,
        ],
        out_specs=[rows, pl.BlockSpec((1, toks), lambda i: (0, 0))],
        out_shape=[
            jax.ShapeDtypeStruct((half, toks), bf16),
            jax.ShapeDtypeStruct((1, toks), f32),
        ],
        cost_estimate=pl.CostEstimate(
            flops=4 * half * toks, bytes_accessed=8 * half * toks, transcendentals=0
        ),
        compiler_params=pltpu.CompilerParams(vmem_limit_bytes=16 * 2**20),
    )(stats, own, scale, product, target_cols)


def on_device(trunk_rows, res_weight, res_bias, lm_weight, next_ids, valid_mask):
    head = lax.axis_index("x")
    ylo, z, core, yhi = (lax.axis_index(a) for a in ("ylo", "z", "core", "yhi"))
    n_x = lax.axis_size("x")
    n_plane = lax.axis_size("ylo") * lax.axis_size("z")
    n_all = n_plane * lax.axis_size("yhi")
    rows, width = trunk_rows.shape
    toks = n_all * rows

    res_own = res_weight[0].T
    cols = res_own.shape[0]
    pair = 2 * cols
    lm_own = lm_weight[0]
    half, vocab_width = lm_own.shape
    res_other = swap(res_own, "core")
    lm_other = swap(lm_own, "core")
    first = core == 0
    res_pair = jnp.concatenate(
        [jnp.where(first, res_own, res_other), jnp.where(first, res_other, res_own)], 0
    )
    bias_own = res_bias[0].astype(f32)
    bias_other = swap(bias_own, "core")
    bias_pair = jnp.concatenate(
        [jnp.where(first, bias_own, bias_other), jnp.where(first, bias_other, bias_own)]
    )

    chip = ylo * lax.axis_size("z") + z
    block = yhi * n_plane + chip
    odd = head % 2
    half_cols = width // 2
    quarter = half_cols // 2
    iota_r = lax.broadcasted_iota(jnp.int32, (pair, half_cols), 0)
    iota_c = lax.broadcasted_iota(jnp.int32, (pair, half_cols), 1)

    select = jnp.concatenate(
        [(iota_r + block * pair == iota_c + side * half_cols).astype(bf16) for side in (0, 1)], 1
    )
    res_aug = jnp.concatenate([res_pair, select], 0)
    near = lax.dynamic_slice_in_dim(res_aug, odd * half_cols, half_cols, 1)
    far = lax.dynamic_slice_in_dim(res_aug, (1 - odd) * half_cols, half_cols, 1)

    def shift(value, step):
        return lax.ppermute(value, "x", [(i, (i + step) % n_x) for i in range(n_x)])

    line = ("ylo", "yhi")
    n_z = lax.axis_size("z")
    n_y = lax.axis_size("ylo") * lax.axis_size("yhi")
    y = yhi * lax.axis_size("ylo") + ylo

    def z_shift(value, step):
        return lax.ppermute(value, "z", [(i, (i + step) % n_z) for i in range(n_z)])

    def line_index(at):
        return at % 2 * 2 + at // 2

    def y_flip(value, flip):
        pairs = [(line_index(i), line_index(i ^ flip)) for i in range(n_y)]
        return lax.ppermute(value, line, pairs)

    def place(buffer, block, at, row=0):
        return lax.dynamic_update_slice(buffer, block[None], (at, row, 0))

    seen = exchange(jnp.broadcast_to(trunk_rows[None], (n_y, rows, width)), line)
    seen = seen.reshape(n_y * rows, width)
    cut = n_y * rows // 2
    up = down = seen
    trunk = place(jnp.zeros((n_z, n_y * rows, width), bf16), seen, z)
    for step in range(1, n_z // 2):
        up, down = z_shift(up, 1), z_shift(down, -1)
        if step == n_z // 2 - 1:
            up, down, res_aug = lax.optimization_barrier((up, down, res_aug))
        trunk = place(trunk, up, (z - step) % n_z)
        trunk = place(trunk, down, (z + step) % n_z)
    up, down = z_shift(up[:cut], 1), z_shift(down[cut:], -1)
    trunk = place(trunk, up, (z + n_z // 2) % n_z)
    trunk = place(trunk, down, (z + n_z // 2) % n_z, cut)
    trunk = trunk.reshape(toks, width)

    def own_tokens(values):
        values = lax.dynamic_slice_in_dim(values, head + 1, 2 * toks)
        values = values.reshape(lax.axis_size("ylo"), n_z, 2, lax.axis_size("yhi"), rows)
        values = lax.dynamic_index_in_dim(values, core, 2, keepdims=False)
        return values.transpose(1, 0, 2, 3).reshape(toks)

    tok_ids = own_tokens(next_ids)
    live = own_tokens(valid_mask).astype(f32)
    scale = loss_scale * jnp.power(jnp.float32(0.8), head.astype(f32)) * live
    lanes = lax.broadcasted_iota(jnp.int32, (1, vocab_width), 1)

    def onehot(owner):
        return (tok_ids - (chip * 2 + owner) * vocab_width)[:, None] == lanes

    hot_own, hot_other = onehot(core), onehot(1 - core)
    target_cols = vocab_product(
        lm_own, lm_other, hot_own.astype(bf16), hot_other.astype(bf16), bf16
    )
    both = dot(res_aug, trunk, ((1,), (1,)))
    pre = both[:pair] + bias_pair[:, None]
    hidden = (both[pair:] + jax.nn.silu(pre)).astype(bf16)
    hidden_half = exchange(
        jnp.broadcast_to(hidden[None], (n_plane, pair, toks)), plane
    ).reshape(half, toks)
    target_cols, hidden_half = lax.optimization_barrier((target_cols, hidden_half))

    logits, coded = vocab_logits(hidden_half, lm_own, lm_other)
    coded = swap(coded, "yhi")
    spots = jnp.stack([tok_ids - (chip * 2 + owner) * vocab_width for owner in (core, 1 - core)], 1)
    logits, rest_own, rest_other, own_stats = local_softmax(logits, coded, spots, n_plane)
    top = own_stats[0, 0]
    exp_own = jnp.exp(logits[:, :vocab_width] - top[:, None])
    exp_other = jnp.exp(logits[:, vocab_width:] - top[:, None])
    stats = exchange(own_stats, plane)
    part_grad = vocab_product(
        lm_own, lm_other, rest_own, rest_other, bf16
    )
    part_grad, ratio = combine(stats, own_stats, scale[None], part_grad, target_cols)
    ratio = ratio[0]
    parts = exchange(part_grad.reshape(n_plane, pair, toks), plane)
    hidden_grad = jnp.sum(parts.astype(f32), axis=0)
    pre_grad = hidden_grad * silu_grad(pre)
    pre_round = pre_grad.astype(bf16)

    def grad_of(exps, hot):
        return jnp.where(hot, ratio[:, None] * exps - scale[:, None], ratio[:, None] * exps).astype(
            bf16
        )

    grad_own = grad_of(exp_own, hot_own)
    grad_other = grad_of(exp_other, hot_other)
    hidden_both = jnp.concatenate([hidden_half, swap(hidden_half, "core")], 1)
    grad_both = jnp.concatenate([grad_own, swap(grad_other, "core")], 0)
    lm_grad = dot(hidden_both, grad_both, ((1,), (0,))).astype(bf16)
    pre_own = lax.dynamic_slice_in_dim(pre_grad, core * cols, cols, 0)
    pre_sibling = swap(lax.dynamic_slice_in_dim(pre_grad, (1 - core) * cols, cols, 0), "core")
    bias_grad = jnp.sum(pre_own, axis=1) + jnp.sum(pre_sibling, axis=1)
    pre_both = jnp.concatenate([pre_own, pre_sibling], 1).astype(bf16)

    trunk_both = jnp.concatenate([trunk, swap(trunk, "core")], 0)
    res_grad = dot(pre_both, trunk_both, ((1,), (0,))).astype(bf16)
    order = lax.broadcasted_iota(jnp.int32, (toks, toks), 1)
    order_y, order_z = order // (rows * n_z), order // rows % n_z
    order = (order_z * n_y + line_index(order_y)) * rows + order % rows
    order = (order == lax.broadcasted_iota(jnp.int32, (toks, toks), 0)).astype(bf16)
    both_grad = jnp.concatenate([pre_round, hidden_grad.astype(bf16)], 0)
    both_grad = dot(both_grad, order, ((1,), (0,))).astype(bf16)
    given = dot(both_grad, far, ((0,), (0,))).astype(bf16)
    got_left = shift(given[:, quarter:], 1)
    got_right = shift(given[:, :quarter], -1)
    keep = dot(both_grad, near, ((0,), (0,)))
    by_x = jnp.concatenate(
        [keep[:, :quarter] + got_right.astype(f32), keep[:, quarter:] + got_left.astype(f32)], 1
    ).astype(bf16)
    by_x = by_x.reshape(n_y, n_z * rows, half_cols)
    by_y = lax.dynamic_index_in_dim(by_x, y, 0, keepdims=False).astype(f32)
    for flip in (1, 3, 2):
        sent = lax.dynamic_index_in_dim(by_x, y ^ flip, 0, keepdims=False)
        pairs = [(line_index(i), line_index(i ^ flip)) for i in range(n_y)]
        got = lax.ppermute(sent, line, pairs)
        by_y = by_y + got.astype(f32)
    by_z = exchange(by_y.astype(bf16).reshape(n_z, rows, half_cols), "z")
    by_z, res_grad = lax.optimization_barrier((by_z, res_grad))
    summed = jnp.sum(by_z.astype(f32), axis=0)
    sent = summed.astype(bf16)
    here = summed + shift(sent, 2).astype(f32)
    there = shift(sent, 1).astype(f32) + shift(sent, -1).astype(f32)
    trunk_grad = jnp.concatenate(
        [jnp.where(odd == 0, here, there), jnp.where(odd == 0, there, here)], 1
    )

    return (trunk_grad, res_grad.T[None], bias_grad[None], lm_grad[None])


def solution(mesh):
    fine = Mesh(mesh.devices.reshape(4, 2, 8, 2, 2), ("x", "ylo", "z", "core", "yhi"))
    vocab = ("ylo", "z", "core")
    in_specs = (
        P((*vocab, "yhi"), None),
        P("x", None, ("yhi", *vocab)),
        P("x", ("yhi", *vocab)),
        P("x", "yhi", vocab),
        P(),
        P(),
    )
    out_specs = (
        P((*vocab, "yhi"), None),
        P("x", None, ("yhi", *vocab)),
        P("x", ("yhi", *vocab)),
        P("x", "yhi", vocab),
    )
    return jax.shard_map(
        on_device, mesh=fine, in_specs=in_specs, out_specs=out_specs, check_vma=False
    )
```

```python
import jax
import jax.numpy as jnp
from jax import lax
from jax.experimental import pallas as pl
from jax.experimental.pallas import tpu as pltpu
from jax.sharding import Mesh
from jax.sharding import PartitionSpec as P

loss_scale = 16.0
int16_top = 32767.0
ln2 = 0.6931471805599453
vmem_bytes = 60 * 2**20
f32 = jnp.float32
bf16 = jnp.bfloat16
plane = ("ylo", "z")
plane_all = ("ylo", "z", "yhi")


def silu_grad(value):
    sigma = jax.nn.sigmoid(value)
    return sigma * (1.0 + value * (1.0 - sigma))


def swap(value, axis):
    return lax.ppermute(value, axis, [(0, 1), (1, 0)])


def exchange(value, axes):
    return lax.all_to_all(value, axes, 0, 0, tiled=True)


def dot(a, b, contract):
    return lax.dot_general(a, b, ((contract[0], contract[1]), ((), ())), preferred_element_type=f32)


def vocab_product(lm_a, lm_b, rows_a, rows_b, dtype):
    half, columns = lm_a.shape
    toks = rows_a.shape[0]
    step = half // 2

    def kernel(a_ref, b_ref, ra_ref, rb_ref, out_ref):
        total = dot(a_ref[...], ra_ref[...], ((1,), (1,)))
        total = total + dot(b_ref[...], rb_ref[...], ((1,), (1,)))
        out_ref[...] = total.astype(out_ref.dtype)

    weights = pl.BlockSpec((step, columns), lambda i: (i, 0))
    whole = pl.BlockSpec((toks, columns), lambda i: (0, 0))
    return pl.pallas_call(
        kernel,
        grid=(half // step,),
        in_specs=[weights, weights, whole, whole],
        out_specs=pl.BlockSpec((step, toks), lambda i: (i, 0)),
        out_shape=jax.ShapeDtypeStruct((half, toks), dtype),
        cost_estimate=pl.CostEstimate(
            flops=4 * half * columns * toks,
            bytes_accessed=4 * half * columns + 4 * half * toks,
            transcendentals=0,
        ),
        compiler_params=pltpu.CompilerParams(vmem_limit_bytes=vmem_bytes),
    )(lm_a, lm_b, rows_a, rows_b)


def vocab_logits(hidden, lm_a, lm_b):
    half, columns = lm_a.shape
    toks = hidden.shape[1]
    step = half // 2
    lanes = 128

    def kernel(h_ref, a_ref, b_ref, out_ref, coded_ref):
        part_a = dot(h_ref[...], a_ref[...], ((0,), (0,)))
        part_b = dot(h_ref[...], b_ref[...], ((0,), (0,)))

        @pl.when(pl.program_id(0) == 0)
        def _():
            out_ref[:, :columns] = part_a
            out_ref[:, columns:] = part_b

        @pl.when(pl.program_id(0) > 0)
        def _():
            value = out_ref[...] + jnp.concatenate([part_a, part_b], 1)
            out_ref[...] = value
            size = jnp.max(jnp.abs(value), axis=1, keepdims=True)
            power = jnp.ceil(jnp.log(jnp.maximum(size, 1e-30)) * (1.0 / ln2))
            code = jnp.floor(value * (int16_top * jnp.exp(power * -ln2)) + 0.5)
            code = jnp.clip(code, -int16_top, int16_top)
            coded_ref[:, : 2 * columns] = code.astype(jnp.int32).astype(jnp.int16)
            power = jnp.broadcast_to(power, (toks, lanes))
            coded_ref[:, 2 * columns :] = power.astype(jnp.int32).astype(jnp.int16)

    weights = pl.BlockSpec((step, columns), lambda i: (i, 0))
    return pl.pallas_call(
        kernel,
        grid=(half // step,),
        in_specs=[pl.BlockSpec((step, toks), lambda i: (i, 0)), weights, weights],
        out_specs=[
            pl.BlockSpec((toks, 2 * columns), lambda i: (0, 0)),
            pl.BlockSpec((toks, 2 * columns + lanes), lambda i: (0, 0)),
        ],
        out_shape=[
            jax.ShapeDtypeStruct((toks, 2 * columns), f32),
            jax.ShapeDtypeStruct((toks, 2 * columns + lanes), jnp.int16),
        ],
        cost_estimate=pl.CostEstimate(
            flops=4 * half * columns * toks,
            bytes_accessed=4 * half * columns + 2 * half * toks,
            transcendentals=0,
        ),
        compiler_params=pltpu.CompilerParams(vmem_limit_bytes=vmem_bytes),
    )(hidden, lm_a, lm_b)


def local_softmax(logits, coded, spots, copies):
    toks, columns = logits.shape
    width = columns // 2

    def kernel(logits_ref, coded_ref, spots_ref, rest_a_ref, rest_b_ref, stats_ref):
        power = coded_ref[:, columns : columns + 1].astype(jnp.int32).astype(f32)
        code = coded_ref[:, :columns].astype(jnp.int32).astype(f32)
        total = logits_ref[...] + code * (jnp.exp(power * ln2) * (1.0 / int16_top))
        top = jnp.max(total, axis=1, keepdims=True)
        rests, targets = 0.0, 0.0
        for side, out_ref in ((0, rest_a_ref), (1, rest_b_ref)):
            exps = jnp.exp(total[:, side * width : (side + 1) * width] - top)
            lanes = lax.broadcasted_iota(jnp.int32, (toks, width), 1)
            hot = lanes == spots_ref[:, side : side + 1]
            rest = jnp.where(hot, 0.0, exps)
            out_ref[...] = rest.astype(bf16)
            rests = rests + jnp.sum(rest, axis=1, keepdims=True)
            targets = targets + jnp.sum(jnp.where(hot, exps, 0.0), axis=1, keepdims=True)
        for row, value in enumerate((top, rests, targets)):
            line = jnp.broadcast_to(value, (toks, toks)).T[0:1]
            stats_ref[:, row, :] = jnp.broadcast_to(line, (copies, toks))

    return pl.pallas_call(
        kernel,
        out_shape=[
            jax.ShapeDtypeStruct((toks, width), bf16),
            jax.ShapeDtypeStruct((toks, width), bf16),
            jax.ShapeDtypeStruct((copies, 3, toks), f32),
        ],
        cost_estimate=pl.CostEstimate(
            flops=12 * toks * columns,
            bytes_accessed=12 * toks * columns,
            transcendentals=toks * columns,
        ),
        compiler_params=pltpu.CompilerParams(vmem_limit_bytes=vmem_bytes),
    )(logits, coded, spots)


def combine(stats, own, scale, product, target_cols):
    half, toks = product.shape
    step = half

    def kernel(stats_ref, own_ref, scale_ref, product_ref, target_ref, out_ref, ratio_ref):
        tops, rests, targets = stats_ref[:, 0, :], stats_ref[:, 1, :], stats_ref[:, 2, :]
        top, scale = own_ref[0:1, 0, :], scale_ref[...]
        all_top = jnp.max(tops, axis=0, keepdims=True)
        weight = jnp.exp(tops - all_top)
        rest = jnp.sum(rests * weight, axis=0, keepdims=True)
        total = rest + jnp.sum(targets * weight, axis=0, keepdims=True)
        ratio = scale * jnp.exp(top - all_top) / total
        ratio_ref[...] = ratio
        value = product_ref[...].astype(f32) * ratio - target_ref[...].astype(f32) * (scale * rest / total)
        out_ref[...] = value.astype(out_ref.dtype)

    rows = pl.BlockSpec((step, toks), lambda i: (i, 0))
    return pl.pallas_call(
        kernel,
        grid=(half // step,),
        in_specs=[
            pl.BlockSpec(stats.shape, lambda i: (0, 0, 0)),
            pl.BlockSpec(own.shape, lambda i: (0, 0, 0)),
            pl.BlockSpec(scale.shape, lambda i: (0, 0)),
            rows,
            rows,
        ],
        out_specs=[rows, pl.BlockSpec((1, toks), lambda i: (0, 0))],
        out_shape=[
            jax.ShapeDtypeStruct((half, toks), bf16),
            jax.ShapeDtypeStruct((1, toks), f32),
        ],
        cost_estimate=pl.CostEstimate(
            flops=4 * half * toks, bytes_accessed=8 * half * toks, transcendentals=0
        ),
        compiler_params=pltpu.CompilerParams(vmem_limit_bytes=16 * 2**20),
    )(stats, own, scale, product, target_cols)


def on_device(trunk_rows, res_weight, res_bias, lm_weight, next_ids, valid_mask):
    head = lax.axis_index("x")
    ylo, z, core, yhi = (lax.axis_index(a) for a in ("ylo", "z", "core", "yhi"))
    n_x = lax.axis_size("x")
    n_plane = lax.axis_size("ylo") * lax.axis_size("z")
    n_all = n_plane * lax.axis_size("yhi")
    rows, width = trunk_rows.shape
    toks = n_all * rows

    res_own = res_weight[0].T
    cols = res_own.shape[0]
    pair = 2 * cols
    lm_own = lm_weight[0]
    half, vocab_width = lm_own.shape
    res_other = swap(res_own, "core")
    lm_other = swap(lm_own, "core")
    first = core == 0
    res_pair = jnp.concatenate(
        [jnp.where(first, res_own, res_other), jnp.where(first, res_other, res_own)], 0
    )
    bias_own = res_bias[0].astype(f32)
    bias_other = swap(bias_own, "core")
    bias_pair = jnp.concatenate(
        [jnp.where(first, bias_own, bias_other), jnp.where(first, bias_other, bias_own)]
    )

    chip = ylo * lax.axis_size("z") + z
    block = yhi * n_plane + chip
    odd = head % 2
    half_cols = width // 2
    quarter = half_cols // 2
    iota_r = lax.broadcasted_iota(jnp.int32, (pair, half_cols), 0)
    iota_c = lax.broadcasted_iota(jnp.int32, (pair, half_cols), 1)

    select = jnp.concatenate(
        [(iota_r + block * pair == iota_c + side * half_cols).astype(bf16) for side in (0, 1)], 1
    )
    res_aug = jnp.concatenate([res_pair, select], 0)
    near = lax.dynamic_slice_in_dim(res_aug, odd * half_cols, half_cols, 1)
    far = lax.dynamic_slice_in_dim(res_aug, (1 - odd) * half_cols, half_cols, 1)

    def shift(value, step):
        return lax.ppermute(value, "x", [(i, (i + step) % n_x) for i in range(n_x)])

    line = ("ylo", "yhi")
    n_z = lax.axis_size("z")
    n_y = lax.axis_size("ylo") * lax.axis_size("yhi")
    y = yhi * lax.axis_size("ylo") + ylo

    def z_shift(value, step):
        return lax.ppermute(value, "z", [(i, (i + step) % n_z) for i in range(n_z)])

    def line_index(at):
        return at % 2 * 2 + at // 2

    def y_flip(value, flip):
        pairs = [(line_index(i), line_index(i ^ flip)) for i in range(n_y)]
        return lax.ppermute(value, line, pairs)

    def place(buffer, block, at, row=0):
        return lax.dynamic_update_slice(buffer, block[None], (at, row, 0))

    seen = exchange(jnp.broadcast_to(trunk_rows[None], (n_y, rows, width)), line)
    seen = seen.reshape(n_y * rows, width)
    cut = n_y * rows // 2
    up = down = seen
    trunk = place(jnp.zeros((n_z, n_y * rows, width), bf16), seen, z)
    for step in range(1, n_z // 2):
        up, down = z_shift(up, 1), z_shift(down, -1)
        if step == n_z // 2 - 1:
            up, down, res_aug = lax.optimization_barrier((up, down, res_aug))
        trunk = place(trunk, up, (z - step) % n_z)
        trunk = place(trunk, down, (z + step) % n_z)
    up, down = z_shift(up[:cut], 1), z_shift(down[cut:], -1)
    trunk = place(trunk, up, (z + n_z // 2) % n_z)
    trunk = place(trunk, down, (z + n_z // 2) % n_z, cut)
    trunk = trunk.reshape(toks, width)

    def own_tokens(values):
        values = lax.dynamic_slice_in_dim(values, head + 1, 2 * toks)
        values = values.reshape(lax.axis_size("ylo"), n_z, 2, lax.axis_size("yhi"), rows)
        values = lax.dynamic_index_in_dim(values, core, 2, keepdims=False)
        return values.transpose(1, 0, 2, 3).reshape(toks)

    tok_ids = own_tokens(next_ids)
    live = own_tokens(valid_mask).astype(f32)
    scale = loss_scale * jnp.power(jnp.float32(0.8), head.astype(f32)) * live
    lanes = lax.broadcasted_iota(jnp.int32, (1, vocab_width), 1)

    def onehot(owner):
        return (tok_ids - (chip * 2 + owner) * vocab_width)[:, None] == lanes

    hot_own, hot_other = onehot(core), onehot(1 - core)
    target_cols = vocab_product(
        lm_own, lm_other, hot_own.astype(bf16), hot_other.astype(bf16), bf16
    )
    both = dot(res_aug, trunk, ((1,), (1,)))
    pre = both[:pair] + bias_pair[:, None]
    hidden = (both[pair:] + jax.nn.silu(pre)).astype(bf16)
    hidden_half = exchange(
        jnp.broadcast_to(hidden[None], (n_plane, pair, toks)), plane
    ).reshape(half, toks)
    target_cols, hidden_half = lax.optimization_barrier((target_cols, hidden_half))

    logits, coded = vocab_logits(hidden_half, lm_own, lm_other)
    coded = swap(coded, "yhi")
    spots = jnp.stack([tok_ids - (chip * 2 + owner) * vocab_width for owner in (core, 1 - core)], 1)
    rest_own, rest_other, own_stats = local_softmax(logits, coded, spots, n_plane)
    top = own_stats[0, 0]
    coded = coded.astype(f32)
    logits = logits + coded[:, : 2 * vocab_width] * (
        jnp.exp(coded[:, 2 * vocab_width : 2 * vocab_width + 1] * ln2) * (1.0 / int16_top)
    )
    exp_own = jnp.exp(logits[:, :vocab_width] - top[:, None])
    exp_other = jnp.exp(logits[:, vocab_width:] - top[:, None])
    stats = exchange(own_stats, plane)
    part_grad = vocab_product(
        lm_own, lm_other, rest_own, rest_other, bf16
    )
    part_grad, ratio = combine(stats, own_stats, scale[None], part_grad, target_cols)
    ratio = ratio[0]
    parts = exchange(part_grad.reshape(n_plane, pair, toks), plane)
    hidden_grad = jnp.sum(parts.astype(f32), axis=0)
    pre_grad = hidden_grad * silu_grad(pre)
    pre_round = pre_grad.astype(bf16)

    def grad_of(exps, hot):
        return jnp.where(hot, ratio[:, None] * exps - scale[:, None], ratio[:, None] * exps).astype(
            bf16
        )

    grad_own = grad_of(exp_own, hot_own)
    grad_other = grad_of(exp_other, hot_other)
    hidden_both = jnp.concatenate([hidden_half, swap(hidden_half, "core")], 1)
    grad_both = jnp.concatenate([grad_own, swap(grad_other, "core")], 0)
    lm_grad = dot(hidden_both, grad_both, ((1,), (0,))).astype(bf16)
    pre_own = lax.dynamic_slice_in_dim(pre_grad, core * cols, cols, 0)
    pre_sibling = swap(lax.dynamic_slice_in_dim(pre_grad, (1 - core) * cols, cols, 0), "core")
    bias_grad = jnp.sum(pre_own, axis=1) + jnp.sum(pre_sibling, axis=1)
    pre_both = jnp.concatenate([pre_own, pre_sibling], 1).astype(bf16)

    trunk_both = jnp.concatenate([trunk, swap(trunk, "core")], 0)
    res_grad = dot(pre_both, trunk_both, ((1,), (0,))).astype(bf16)
    order = lax.broadcasted_iota(jnp.int32, (toks, toks), 1)
    order_y, order_z = order // (rows * n_z), order // rows % n_z
    order = (order_z * n_y + line_index(order_y)) * rows + order % rows
    order = (order == lax.broadcasted_iota(jnp.int32, (toks, toks), 0)).astype(bf16)
    both_grad = jnp.concatenate([pre_round, hidden_grad.astype(bf16)], 0)
    both_grad = dot(both_grad, order, ((1,), (0,))).astype(bf16)
    given = dot(both_grad, far, ((0,), (0,))).astype(bf16)
    got_left = shift(given[:, quarter:], 1)
    got_right = shift(given[:, :quarter], -1)
    keep = dot(both_grad, near, ((0,), (0,)))
    by_x = jnp.concatenate(
        [keep[:, :quarter] + got_right.astype(f32), keep[:, quarter:] + got_left.astype(f32)], 1
    ).astype(bf16)
    by_x = by_x.reshape(n_y, n_z * rows, half_cols)
    by_y = lax.dynamic_index_in_dim(by_x, y, 0, keepdims=False).astype(f32)
    for flip in (1, 3, 2):
        sent = lax.dynamic_index_in_dim(by_x, y ^ flip, 0, keepdims=False)
        pairs = [(line_index(i), line_index(i ^ flip)) for i in range(n_y)]
        got = lax.ppermute(sent, line, pairs)
        by_y = by_y + got.astype(f32)
    by_z = exchange(by_y.astype(bf16).reshape(n_z, rows, half_cols), "z")
    by_z, res_grad = lax.optimization_barrier((by_z, res_grad))
    summed = jnp.sum(by_z.astype(f32), axis=0)
    sent = summed.astype(bf16)
    here = summed + shift(sent, 2).astype(f32)
    there = shift(sent, 1).astype(f32) + shift(sent, -1).astype(f32)
    trunk_grad = jnp.concatenate(
        [jnp.where(odd == 0, here, there), jnp.where(odd == 0, there, here)], 1
    )

    return (trunk_grad, res_grad.T[None], bias_grad[None], lm_grad[None])


def solution(mesh):
    fine = Mesh(mesh.devices.reshape(4, 2, 8, 2, 2), ("x", "ylo", "z", "core", "yhi"))
    vocab = ("ylo", "z", "core")
    in_specs = (
        P((*vocab, "yhi"), None),
        P("x", None, ("yhi", *vocab)),
        P("x", ("yhi", *vocab)),
        P("x", "yhi", vocab),
        P(),
        P(),
    )
    out_specs = (
        P((*vocab, "yhi"), None),
        P("x", None, ("yhi", *vocab)),
        P("x", ("yhi", *vocab)),
        P("x", "yhi", vocab),
    )
    return jax.shard_map(
        on_device, mesh=fine, in_specs=in_specs, out_specs=out_specs, check_vma=False
    )
```
